32 devices in a mesh: groups: 2 (over y), seq: 8 (over z, x), head: 2 (over core).
Axes of the slice: x: 2, y: 2, z: 4, core: 2. Of those that a mesh axis runs over, the one named last changes fastest.
Arguments:
- query_states: bfloat16 [2048, 1536], P(('groups', 'seq'), 'head'), parts along dimension 0, may hold values from -8 to 8
- key_states: bfloat16 [2048, 1536], P(('groups', 'seq'), 'head'), parts along dimension 0, may hold values from -8 to 8
- value_states: bfloat16 [2048, 1536], P(('groups', 'seq'), 'head'), parts along dimension 0, may hold values from -6 to 6
- d_attended: bfloat16 [2048, 1536], P(('groups', 'seq'), 'head'), parts along dimension 0, may hold values from -6 to 6
- ctrl_key: bfloat16 [512, 1536], P(('groups', 'seq'), 'head'), parts along dimension 0, may hold values from -6 to 6
- ctrl_value: bfloat16 [512, 1536], P(('groups', 'seq'), 'head'), parts along dimension 0, may hold values from -6 to 6
- ctrl_bias: float32 [24], P('head'), may hold values from 0.5 to 3
- tube_lengths: int32 [8], P('groups'), parts along dimension 0, may hold values from 1 to 3, as said below
- tube_owner: int32 [8], P('groups'), parts along dimension 0, may hold values from 0 to 7
- ctrl_owner: int32 [512], P('groups'), parts along dimension 0, may hold values from 0 to 7
Outputs:
- attended: bfloat16 [2048, 1536], P(('groups', 'seq'), 'head'), parts along dimension 0
- d_query: bfloat16 [2048, 1536], P(('groups', 'seq'), 'head'), parts along dimension 0
- d_key: bfloat16 [2048, 1536], P(('groups', 'seq'), 'head'), parts along dimension 0
- d_value: bfloat16 [2048, 1536], P(('groups', 'seq'), 'head'), parts along dimension 0
- d_ctrl_key: bfloat16 [512, 1536], P(('groups', 'seq'), 'head'), parts along dimension 0
- d_ctrl_value: bfloat16 [512, 1536], P(('groups', 'seq'), 'head'), parts along dimension 0
The draws below stay inside these ranges and needn't reach their ends.
There are 2 independent parts, one for each index of `groups`. The reference program is written for one: setup_inputs(seed, part) draws one part's arguments, and reference() takes and returns one part's arrays. A program takes and returns all parts, laid end to end along the dimension named above; an argument that names none is the same for every part. Nothing has to cross between parts.
Inputs may be any that keep to these rules, and one draw needn't show every extreme that they name: Tube t is the run of tube_lengths[t] consecutive blocks of 128 tokens after the blocks of the tubes before it; the lengths sum to 8 and the longest has exactly 3 blocks.
All inputs are finite; a program needn't handle non-finite values.
Results may differ from the reference program's by a relative error of at most 0.015.
Values may be sent and summed in bfloat16 or wider, within the bound.
A program may use at most 64 MiB of HBM per device.

```python
import jax
import jax.numpy as jnp
from jax import lax

HD = 64
HEADS = 24
BLK = 128
KMAX = 3
CTRL = 256
INST = 8
TOK_DEV = 128
TOKENS = 1024
NBLK = 8
TUBES = 4
N_SEQ = 8


def draw_query_states(key, part):
    key = jax.random.fold_in(key, 5)
    array_shape = (TOKENS, HEADS * HD)
    entries = jax.random.truncated_normal(key, -4.0, 4.0, array_shape, dtype=jnp.float32)
    return entries.astype(jnp.bfloat16)


def draw_key_states(key, part):
    key = jax.random.fold_in(key, 7)
    array_shape = (TOKENS, HEADS * HD)
    entries = jax.random.truncated_normal(key, -4.0, 4.0, array_shape, dtype=jnp.float32)
    return entries.astype(jnp.bfloat16)


def draw_tube_lengths(key, part):
    key = jax.random.fold_in(key, 11)
    pick_key, slot_key = jax.random.split(key)
    longest = jax.random.randint(pick_key, (), 0, TUBES)
    slot_total = (TUBES - 1) * (KMAX - 1)
    order = jax.random.permutation(slot_key, jnp.arange(slot_total, dtype=jnp.int32))
    filled = (order < NBLK - TUBES - (KMAX - 1)).astype(jnp.int32)
    slot_tube = jnp.arange(slot_total, dtype=jnp.int32) // (KMAX - 1)
    others = 1 + jnp.sum(jnp.where(slot_tube[None, :] == jnp.arange(TUBES - 1, dtype=jnp.int32)[:, None], filled[None, :], 0), axis=1, dtype=jnp.int32)
    tube_ids = jnp.arange(TUBES, dtype=jnp.int32)
    lower = jnp.concatenate([others, jnp.zeros((1,), jnp.int32)])
    upper = jnp.concatenate([jnp.zeros((1,), jnp.int32), others])
    lengths = jnp.where(tube_ids < longest, lower, jnp.where(tube_ids == longest, KMAX, upper))
    return lengths.astype(jnp.int32)


def with_ends(drawn, rng, low, high):
    spot = [jax.random.randint(jax.random.fold_in(rng, axis), (), 0, length) for axis, length in enumerate(drawn.shape)]
    widest = drawn.shape.index(max(drawn.shape))
    beside = spot[:widest] + [(spot[widest] + 1) % drawn.shape[widest]] + spot[widest + 1:]
    return drawn.at[tuple(spot)].set(low).at[tuple(beside)].set(high)


def shard_levels(stream_key, shape, cuts, low, largest):
    gain = 1.0
    for dim, shards_of in cuts:
        draws = jax.random.uniform(jax.random.fold_in(jax.random.fold_in(stream_key, 6), dim), (shards_of,), jnp.float32, low / len(cuts), largest / len(cuts))
        gain = gain * jnp.repeat(jnp.exp(draws), shape[dim] // shards_of).reshape((-1,) + (1,) * (len(shape) - 1 - dim))
    return gain


def scatter_about(stream_key, extent, scale, limit, pieces=(), held_as=jnp.bfloat16):
    drawn = scale * jax.random.normal(stream_key, extent, jnp.float32)
    if pieces:
        drawn = drawn * shard_levels(stream_key, extent, pieces, -0.22, 0.18)
    return jnp.clip(drawn, -limit, limit).astype(held_as)


def setup_inputs(seed: int = 0, part: int = 0) -> dict:
    keys = jax.random.split(jax.random.key(seed), 11)
    own_keys = jax.random.split(jax.random.fold_in(keys[10], part), 11)
    return {
        "query_states": draw_query_states(jax.random.fold_in(jax.random.fold_in(keys[10], part), 71), part),
        "key_states": draw_key_states(jax.random.fold_in(jax.random.fold_in(keys[10], part), 71), part),
        "value_states": scatter_about(own_keys[2], (TOKENS, HEADS * HD), 1.0, 6.0, ((0, 8), (1, 2))),
        "d_attended": scatter_about(own_keys[3], (TOKENS, HEADS * HD), 1.0, 6.0, ((0, 8), (1, 2))),
        "ctrl_key": scatter_about(own_keys[4], (CTRL, HEADS * HD), 1.0, 6.0, ((0, 8), (1, 2))),
        "ctrl_value": scatter_about(own_keys[5], (CTRL, HEADS * HD), 1.0, 6.0, ((0, 8), (1, 2))),
        "ctrl_bias": jnp.clip(0.5 + 2.5 * jax.random.uniform(keys[6], (HEADS,), jnp.float32) ** shard_levels(keys[6], (HEADS,), ((0, 2),), -0.2, 0.2), 0.5, 3.0),
        "tube_lengths": draw_tube_lengths(jax.random.fold_in(jax.random.fold_in(keys[10], part), 71), part),
        "tube_owner": with_ends(jax.random.randint(own_keys[8], (TUBES,), 0, INST), jax.random.fold_in(own_keys[8], 1), 0, INST - 1).astype(jnp.int32),
        "ctrl_owner": with_ends(jax.random.randint(own_keys[9], (CTRL,), 0, INST), jax.random.fold_in(own_keys[9], 1), 0, INST - 1).astype(jnp.int32),
    }


MASKED = -1.0e30


def round_trip(values):
    return lax.optimization_barrier(values.astype(jnp.bfloat16)).astype(jnp.float32)


def reference(query_states, key_states, value_states, d_attended, ctrl_key, ctrl_value, ctrl_bias, tube_lengths, tube_owner, ctrl_owner):
    width_all = query_states.shape[1]
    head_count = width_all // HD
    head_scale = HD ** -0.5
    per_device = TOK_DEV // BLK
    tube_ends = jnp.cumsum(tube_lengths, dtype=jnp.int32)
    blocks = jnp.arange(NBLK, dtype=jnp.int32)
    tube_index = jnp.sum((tube_ends[None, :] <= blocks[:, None]).astype(jnp.int32), axis=1, dtype=jnp.int32)
    matches = jnp.arange(TUBES, dtype=jnp.int32)[None, :] == tube_index[:, None]
    owner_index = jnp.sum(jnp.where(matches, tube_owner[None, :], 0), axis=1, dtype=jnp.int32)
    block_start = jnp.sum(jnp.where(matches, (tube_ends - tube_lengths)[None, :], 0), axis=1, dtype=jnp.int32)
    ctrl_keys = ctrl_key.astype(jnp.float32).reshape(CTRL, head_count, HD)
    ctrl_values = ctrl_value.astype(jnp.float32).reshape(CTRL, head_count, HD)
    ctrl_shift = ctrl_bias.astype(jnp.float32)[:, None, None]
    window_rows = KMAX * BLK
    buffer_rows = (per_device + 2 * (KMAX - 1)) * BLK
    pad_rows = (KMAX - 1) * BLK

    def device_step(carried, device):
        key_pad, value_pad, ctrl_key_grad, ctrl_value_grad = carried
        key_buffer = jnp.zeros((buffer_rows, head_count, HD), jnp.float32)
        value_buffer = jnp.zeros((buffer_rows, head_count, HD), jnp.float32)
        attended_rows, d_query_rows = [], []
        for query_local in range(per_device):
            block_id = (device * per_device + query_local).astype(jnp.int32)
            q_blk = lax.dynamic_slice_in_dim(query_states, block_id * BLK, BLK).astype(jnp.float32).reshape(BLK, head_count, HD)
            g_blk = lax.dynamic_slice_in_dim(d_attended, block_id * BLK, BLK).astype(jnp.float32).reshape(BLK, head_count, HD)
            first_block = jnp.minimum(block_start[block_id], NBLK - KMAX).astype(jnp.int32)
            k_win = lax.dynamic_slice_in_dim(key_states, first_block * BLK, window_rows).astype(jnp.float32).reshape(window_rows, head_count, HD)
            v_win = lax.dynamic_slice_in_dim(value_states, first_block * BLK, window_rows).astype(jnp.float32).reshape(window_rows, head_count, HD)
            key_tubes = lax.dynamic_slice_in_dim(tube_index, first_block, KMAX)
            key_mask = jnp.repeat(key_tubes == tube_index[block_id], BLK)[None, None, :]
            ctrl_mask = (ctrl_owner == owner_index[block_id])[None, None, :]
            tube_scores = jnp.where(key_mask, jnp.einsum("qhd,khd->hqk", q_blk, k_win) * head_scale, MASKED)
            ctrl_scores = jnp.where(ctrl_mask, jnp.einsum("qhd,khd->hqk", q_blk, ctrl_keys) * head_scale + ctrl_shift, MASKED)
            scores = jnp.concatenate([tube_scores, ctrl_scores], axis=-1)
            row_high = jnp.max(scores, axis=-1, keepdims=True)
            weights = jnp.exp(scores - row_high) / jnp.sum(jnp.exp(scores - row_high), axis=-1, keepdims=True)
            rounded = round_trip(weights)
            keys_all = jnp.concatenate([k_win, ctrl_keys], axis=0)
            values_all = jnp.concatenate([v_win, ctrl_values], axis=0)
            attended_f = round_trip(jnp.einsum("hqk,khd->qhd", rounded, values_all))
            row_delta = jnp.sum(g_blk * attended_f, axis=-1).T[:, :, None]
            d_prob = jnp.einsum("qhd,khd->hqk", g_blk, values_all)
            d_scores = round_trip(weights * (d_prob - row_delta))
            d_query_blk = jnp.einsum("hqk,khd->qhd", d_scores, keys_all) * head_scale
            key_grad = jnp.einsum("hqk,qhd->khd", d_scores[..., :window_rows], q_blk) * head_scale
            value_grad = jnp.einsum("hqk,qhd->khd", rounded[..., :window_rows], g_blk)
            ctrl_key_grad = ctrl_key_grad + jnp.einsum("hqk,qhd->khd", d_scores[..., window_rows:], q_blk) * head_scale
            ctrl_value_grad = ctrl_value_grad + jnp.einsum("hqk,qhd->khd", rounded[..., window_rows:], g_blk)
            offset = ((first_block - device * per_device + KMAX - 1) * BLK).astype(jnp.int32)
            key_buffer = lax.dynamic_update_slice_in_dim(key_buffer, lax.dynamic_slice_in_dim(key_buffer, offset, window_rows) + key_grad, offset, 0)
            value_buffer = lax.dynamic_update_slice_in_dim(value_buffer, lax.dynamic_slice_in_dim(value_buffer, offset, window_rows) + value_grad, offset, 0)
            attended_rows.append(attended_f.astype(jnp.bfloat16).reshape(BLK, width_all))
            d_query_rows.append(d_query_blk.astype(jnp.bfloat16).reshape(BLK, width_all))
        start_row = (device * per_device * BLK).astype(jnp.int32)
        key_pad = lax.dynamic_update_slice_in_dim(key_pad, lax.dynamic_slice_in_dim(key_pad, start_row, buffer_rows) + round_trip(key_buffer), start_row, 0)
        value_pad = lax.dynamic_update_slice_in_dim(value_pad, lax.dynamic_slice_in_dim(value_pad, start_row, buffer_rows) + round_trip(value_buffer), start_row, 0)
        return (key_pad, value_pad, ctrl_key_grad, ctrl_value_grad), (jnp.concatenate(attended_rows, axis=0), jnp.concatenate(d_query_rows, axis=0))

    padded_rows = (NBLK + 2 * (KMAX - 1)) * BLK
    initial = (jnp.zeros((padded_rows, head_count, HD), jnp.float32), jnp.zeros((padded_rows, head_count, HD), jnp.float32),
               jnp.zeros((CTRL, head_count, HD), jnp.float32), jnp.zeros((CTRL, head_count, HD), jnp.float32))
    final_state, stacked = lax.scan(device_step, initial, jnp.arange(N_SEQ, dtype=jnp.int32))
    key_pad, value_pad, ctrl_key_grad, ctrl_value_grad = final_state
    attended = stacked[0].reshape(TOKENS, width_all)
    d_query = stacked[1].reshape(TOKENS, width_all)
    d_key = key_pad[pad_rows:pad_rows + TOKENS].reshape(TOKENS, width_all).astype(jnp.bfloat16)
    d_value = value_pad[pad_rows:pad_rows + TOKENS].reshape(TOKENS, width_all).astype(jnp.bfloat16)
    d_ctrl_key = ctrl_key_grad.reshape(CTRL, width_all).astype(jnp.bfloat16)
    d_ctrl_value = ctrl_value_grad.reshape(CTRL, width_all).astype(jnp.bfloat16)
    return (attended, d_query, d_key, d_value, d_ctrl_key, d_ctrl_value)
```

```python
from functools import partial

import jax
import jax.numpy as jnp
from jax import lax
from jax.experimental import pallas as pl
from jax.experimental.pallas import tpu as pltpu
from jax.sharding import PartitionSpec as P

BLK = 128
REACH = 2


MASKED = -1e30


def passed_along(block, axis, distance):
    devices = range(lax.axis_size(axis))
    route = [(i - distance, i) for i in devices if i - distance in devices]
    return lax.ppermute(block, axis, route)


def tube_tables(tube_lengths, tube_owner, blocks_all):
    tube_ends = jnp.cumsum(tube_lengths, dtype=jnp.int32)
    blocks = jnp.arange(blocks_all, dtype=jnp.int32)
    tube_index = jnp.sum(
        (tube_ends[None, :] <= blocks[:, None]).astype(jnp.int32), axis=1, dtype=jnp.int32
    )
    tube_ids = jnp.arange(tube_lengths.shape[0], dtype=jnp.int32)
    matches = tube_ids[None, :] == tube_index[:, None]
    owner_index = jnp.sum(jnp.where(matches, tube_owner[None, :], 0), axis=1, dtype=jnp.int32)
    return (tube_index, owner_index)


def split_heads(rows_in, head_width):
    return rows_in.reshape(rows_in.shape[0], rows_in.shape[1] // head_width, head_width)


def scores_of(q_blk, k_blk):
    return jnp.einsum(
        "qhd,khd->hqk", q_blk, k_blk, preferred_element_type=jnp.float32
    ) * q_blk.shape[-1] ** (-0.5)


def weights_of(scores, row_high, row_total):
    return jnp.exp(scores - row_high[..., None]) / row_total[..., None]


def raise_stats(statistics, scores):
    row_high, row_total = statistics
    new_high = jnp.maximum(row_high, jnp.max(scores, axis=-1))
    row_total = row_total * jnp.exp(row_high - new_high) + jnp.sum(
        jnp.exp(scores - new_high[..., None]), axis=-1
    )
    return (new_high, row_total)


def unchanged(carried):
    return carried


def round_trip(values):
    return lax.optimization_barrier(values.astype(jnp.bfloat16)).astype(jnp.float32)


def shards(
    query_states,
    key_states,
    value_states,
    d_attended,
    ctrl_key,
    ctrl_value,
    ctrl_bias,
    tube_lengths,
    tube_owner,
    ctrl_owner,
):
    row_count, width_all = query_states.shape
    head_width = width_all // ctrl_bias.shape[0]
    head_scale = head_width ** (-0.5)
    per_device = row_count // BLK
    blocks_all = lax.axis_size("seq") * per_device
    position = lax.axis_index("seq")
    slot_count = 2 * REACH + 1
    tube_index, owner_index = tube_tables(tube_lengths, tube_owner, blocks_all)
    ctrl_pair = lax.all_gather(jnp.stack([ctrl_key, ctrl_value]), "seq", axis=1, tiled=True)
    ctrl_keys = split_heads(ctrl_pair[0], head_width)
    ctrl_values = split_heads(ctrl_pair[1], head_width)
    ctrl_shift = ctrl_bias[:, None, None]
    key_value = jnp.stack([key_states, value_states])
    lower_side = [passed_along(key_value, "seq", distance) for distance in range(REACH, 0, -1)]
    upper_side = [passed_along(key_value, "seq", -distance) for distance in range(1, REACH + 1)]
    kv_window = lower_side + [key_value] + upper_side

    def member(slot_index, block_local, tube_id):
        block_id = (position - REACH + slot_index) * per_device + block_local
        clipped = jnp.clip(block_id, 0, blocks_all - 1)
        return (block_id >= 0) & (block_id < blocks_all) & (tube_index[clipped] == tube_id)

    def window_block(window, slot_index, block_local, member_index):
        return split_heads(
            window[slot_index][member_index, block_local * BLK : (block_local + 1) * BLK],
            head_width,
        )

    def visit_keys(update, carried, tube_id, skipped):
        for slot_index in range(slot_count):
            for key_local in range(per_device):
                if slot_index == REACH and key_local == skipped:
                    continue
                carried = lax.cond(
                    member(slot_index, key_local, tube_id),
                    partial(update, slot_index=slot_index, key_local=key_local),
                    unchanged,
                    carried,
                )
        return carried

    q_blocks, g_blocks, query_tubes, ctrl_masks = ([], [], [], [])
    query_local = 0
    q_blocks.append(split_heads(query_states, head_width))
    g_blocks.append(split_heads(d_attended, head_width))
    block_id = position * per_device + query_local
    query_tubes.append(tube_index[block_id])
    ctrl_masks.append((ctrl_owner == owner_index[block_id])[None, None, :])

    def ctrl_scores(query_local):
        return jnp.where(
            ctrl_masks[query_local],
            scores_of(q_blocks[query_local], ctrl_keys) + ctrl_shift,
            MASKED,
        )

    highs, totals, deltas, attended_blocks = ([], [], [], [])
    query_local = 0
    q_blk = q_blocks[query_local]
    own_scores = scores_of(q_blk, window_block(kv_window, REACH, query_local, 0))
    row_high = jnp.max(own_scores, axis=-1)
    statistics = (row_high, jnp.sum(jnp.exp(own_scores - row_high[..., None]), axis=-1))
    statistics = raise_stats(statistics, ctrl_scores(query_local))

    def add_stats(carried, slot_index, key_local, q_blk=q_blk):
        return raise_stats(
            carried, scores_of(q_blk, window_block(kv_window, slot_index, key_local, 0))
        )

    row_high, row_total = visit_keys(add_stats, statistics, query_tubes[query_local], query_local)
    ctrl_weights = weights_of(ctrl_scores(query_local), row_high, row_total).astype(jnp.bfloat16)
    summed = jnp.einsum(
        "hqk,khd->qhd", ctrl_weights, ctrl_values, preferred_element_type=jnp.float32
    )

    def add_values(
        carried, slot_index, key_local, q_blk=q_blk, row_high=row_high, row_total=row_total
    ):
        k_blk = window_block(kv_window, slot_index, key_local, 0)
        v_blk = window_block(kv_window, slot_index, key_local, 1)
        weights = weights_of(scores_of(q_blk, k_blk), row_high, row_total).astype(jnp.bfloat16)
        return carried + jnp.einsum(
            "hqk,khd->qhd", weights, v_blk, preferred_element_type=jnp.float32
        )

    summed = visit_keys(add_values, summed, query_tubes[query_local], -1)
    attended_blk = summed.astype(jnp.bfloat16)
    row_delta = jnp.sum(
        g_blocks[query_local].astype(jnp.float32) * attended_blk.astype(jnp.float32), axis=-1
    ).T
    highs.append(row_high)
    totals.append(row_total)
    deltas.append(row_delta)
    attended_blocks.append(attended_blk)

    def grad_terms(query_local, v_blk, scores):
        weights = weights_of(scores, highs[query_local], totals[query_local])
        d_prob = jnp.einsum(
            "qhd,khd->hqk", g_blocks[query_local], v_blk, preferred_element_type=jnp.float32
        )
        d_scores = (weights * (d_prob - deltas[query_local][..., None])).astype(jnp.bfloat16)
        return (weights.astype(jnp.bfloat16), d_scores)

    query_local = 0
    rounded, d_scores = grad_terms(query_local, ctrl_values, ctrl_scores(query_local))
    d_queries = [
        jnp.einsum("hqk,khd->qhd", d_scores, ctrl_keys, preferred_element_type=jnp.float32)
        * head_scale
    ]
    ctrl_key_grad = (
        jnp.einsum(
            "hqk,qhd->khd", d_scores, q_blocks[query_local], preferred_element_type=jnp.float32
        )
        * head_scale
    )
    ctrl_value_grad = jnp.einsum(
        "hqk,qhd->khd", rounded, g_blocks[query_local], preferred_element_type=jnp.float32
    )
    block_zeros = jnp.zeros((BLK, width_all // head_width, head_width), jnp.float32)
    key_parts = jnp.zeros((2, row_count, width_all), jnp.float32)
    for slot_index in range(slot_count):
        key_local = 0
        k_blk = window_block(kv_window, slot_index, key_local, 0)
        v_blk = window_block(kv_window, slot_index, key_local, 1)
        key_grad = block_zeros
        value_grad = block_zeros
        query_local = 0

        def add_grads(carried, query_local=query_local, k_blk=k_blk, v_blk=v_blk):
            rounded, d_scores = grad_terms(
                query_local, v_blk, scores_of(q_blocks[query_local], k_blk)
            )
            d_query_blk = (
                carried[0]
                + jnp.einsum("hqk,khd->qhd", d_scores, k_blk, preferred_element_type=jnp.float32)
                * head_scale
            )
            key_term = (
                jnp.einsum(
                    "hqk,qhd->khd",
                    d_scores,
                    q_blocks[query_local],
                    preferred_element_type=jnp.float32,
                )
                * head_scale
            )
            value_term = jnp.einsum(
                "hqk,qhd->khd", rounded, g_blocks[query_local], preferred_element_type=jnp.float32
            )
            return (d_query_blk, key_term, value_term)

        carried = lax.cond(
            member(slot_index, key_local, query_tubes[query_local]),
            add_grads,
            unchanged,
            (d_queries[query_local], key_grad, value_grad),
        )
        d_queries[query_local], key_grad, value_grad = carried
        slot_pieces = jnp.stack([key_grad, value_grad]).reshape(2, BLK, width_all)
        if slot_index == REACH:
            key_parts = key_parts + round_trip(slot_pieces)
        else:
            received = passed_along(slot_pieces.astype(jnp.bfloat16), "seq", slot_index - REACH)
            key_parts = key_parts + received.astype(jnp.float32)
    key_results = key_parts.astype(jnp.bfloat16)
    ctrl_terms = jnp.stack(
        [ctrl_key_grad.reshape(-1, width_all), ctrl_value_grad.reshape(-1, width_all)]
    )
    ctrl_results = lax.psum_scatter(ctrl_terms, "seq", scatter_dimension=1, tiled=True).astype(
        jnp.bfloat16
    )
    attended = attended_blocks[0].reshape(row_count, width_all)
    d_query = d_queries[0].reshape(row_count, width_all).astype(jnp.bfloat16)
    return (attended, d_query, key_results[0], key_results[1], ctrl_results[0], ctrl_results[1])


MESH = pl.DeviceIdType.MESH
SLOTS = (-2, -1, 1, 2)
LANES = 128


def masked_pair(rows, low_lanes, factor):
    first = low_lanes.astype(jnp.float32) * factor
    second = factor - first
    return jnp.concatenate(
        [rows * first.astype(rows.dtype), rows * second.astype(rows.dtype)], axis=0
    )


def dot(left, right, left_dim, right_dim):
    return lax.dot_general(
        left, right, (((left_dim,), (right_dim,)), ((), ())), preferred_element_type=jnp.float32
    )


def tube_kernel(
    count, q_ref, k_ref, v_ref, g_ref, ck_ref, cv_ref, bias_ref, flag_ref,
    att_ref, dq_ref, dk_ref, dv_ref, dck_ref, dcv_ref,
    own, window, ctrl, own_grad, grad_out, grad_in, ctrl_out, ctrl_in,
    kv_send, kv_recv, ctrl_send, ctrl_recv, grad_send, grad_recv, sum_send, sum_recv,
):
    me = lax.axis_index("seq")
    rows = q_ref.shape[0]
    ctrl_rows = ck_ref.shape[0]
    pairs = q_ref.shape[1] // LANES
    low_lanes = lax.broadcasted_iota(jnp.int32, (1, LANES), 1) < LANES // 2

    def inside(device):
        return (device >= 0) & (device < count)

    def columns(pair):
        return pl.ds(pl.multiple_of(pair * LANES, LANES), LANES)

    def kv_copy(pair, slot):
        return pltpu.make_async_remote_copy(
            own.at[pair], window.at[pair, slot], kv_send.at[pair, slot], kv_recv.at[pair, slot],
            device_id={"seq": me - SLOTS[slot]}, device_id_type=MESH,
        )

    def grad_copy(pair, slot):
        return pltpu.make_async_remote_copy(
            grad_out.at[pair, slot], grad_in.at[pair, slot],
            grad_send.at[pair, slot], grad_recv.at[pair, slot],
            device_id={"seq": me + SLOTS[slot]}, device_id_type=MESH,
        )

    def ctrl_copy(pair, step):
        return pltpu.make_async_remote_copy(
            ctrl.at[pair, me], ctrl.at[pair, me], ctrl_send.at[pair, step], ctrl_recv.at[pair, step],
            device_id={"seq": lax.rem(me + step, count)}, device_id_type=MESH,
        )

    def ctrl_arrival(pair, step):
        source = lax.rem(me - step + count, count)
        return pltpu.make_async_remote_copy(
            ctrl.at[pair, source], ctrl.at[pair, source],
            ctrl_send.at[pair, step], ctrl_recv.at[pair, step],
            device_id={"seq": source}, device_id_type=MESH,
        )

    def sum_copy(pair, step):
        target = lax.rem(me + step, count)
        return pltpu.make_async_remote_copy(
            ctrl_out.at[pair, target], ctrl_in.at[pair, me],
            sum_send.at[pair, step], sum_recv.at[pair, step],
            device_id={"seq": target}, device_id_type=MESH,
        )

    def sum_arrival(pair, step):
        source = lax.rem(me - step + count, count)
        return pltpu.make_async_remote_copy(
            ctrl_out.at[pair, source], ctrl_in.at[pair, source],
            sum_send.at[pair, step], sum_recv.at[pair, step],
            device_id={"seq": source}, device_id_type=MESH,
        )

    def pack(pair, _):
        own[pair, 0] = k_ref[:, columns(pair)]
        own[pair, 1] = v_ref[:, columns(pair)]
        ctrl[pair, me, 0] = ck_ref[:, columns(pair)]
        ctrl[pair, me, 1] = cv_ref[:, columns(pair)]
        return 0

    lax.fori_loop(0, pairs, pack, 0)
    for slot, distance in enumerate(SLOTS):
        @pl.when(jnp.logical_not(inside(me + distance)))
        def _():
            window[:, slot] = jnp.zeros((pairs,) + window.shape[2:], window.dtype)

        @pl.when(jnp.logical_not(inside(me - distance)))
        def _():
            grad_in[:, slot] = jnp.zeros((pairs,) + grad_in.shape[2:], grad_in.dtype)

    barrier = pltpu.get_barrier_semaphore()
    for step in range(1, count):
        pl.semaphore_signal(
            barrier, inc=1, device_id={"seq": lax.rem(me + step, count)}, device_id_type=MESH
        )
    pl.semaphore_wait(barrier, count - 1)

    def send(pair, _):
        for step in range(1, count):
            ctrl_copy(pair, step).start()
        for slot, distance in enumerate(SLOTS):
            @pl.when(inside(me - distance))
            def _():
                kv_copy(pair, slot).start()
        return 0

    lax.fori_loop(0, pairs, send, 0)

    lower, lower2, upper, upper2 = (flag_ref[i] > 0 for i in (1, 0, 2, 3))
    zero_block = jnp.zeros((rows, LANES), jnp.bfloat16)
    zero_grad = jnp.zeros((rows, LANES), jnp.float32)

    def work(pair, _):
        for step in range(1, count):
            ctrl_arrival(pair, step).wait_recv()
        for slot, distance in enumerate(SLOTS):
            @pl.when(inside(me + distance))
            def _():
                kv_copy(pair, slot).wait_recv()

        def gathered(kind):
            first = jnp.where(
                lower, window[pair, 1, kind], jnp.where(upper2, window[pair, 3, kind], zero_block)
            )
            second = jnp.where(
                upper, window[pair, 2, kind], jnp.where(lower2, window[pair, 0, kind], zero_block)
            )
            shared = ctrl[pair, :, kind].reshape(count * ctrl_rows, LANES)
            return jnp.concatenate([first, own[pair, kind], second, shared], axis=0)

        keys = gathered(0)
        values = gathered(1)
        q_two = masked_pair(q_ref[:, columns(pair)], low_lanes, 0.125)
        g_two = masked_pair(g_ref[:, columns(pair)], low_lanes, 1.0)
        scores = dot(q_two, keys, 1, 1)
        bias = bias_ref[pair]
        scores = jnp.concatenate(
            [scores[:rows] + bias[0:1], scores[rows:] + bias[1:2]], axis=0
        )
        raised = jnp.exp(scores - jnp.max(scores, axis=1, keepdims=True))
        weights = raised * (1.0 / jnp.sum(raised, axis=1, keepdims=True))
        rounded = weights.astype(jnp.bfloat16)
        out_two = dot(rounded, values, 1, 0)
        attended = jnp.where(low_lanes, out_two[:rows], out_two[rows:]).astype(jnp.bfloat16)
        att_ref[:, columns(pair)] = attended
        attended = attended.astype(jnp.float32)
        delta = jnp.sum(
            g_two.astype(jnp.float32) * jnp.concatenate([attended, attended], axis=0),
            axis=1, keepdims=True,
        )
        d_scores = (weights * (dot(g_two, values, 1, 1) - delta)).astype(jnp.bfloat16)
        dq_two = dot(d_scores, keys, 1, 0) * 0.125
        dq_ref[:, columns(pair)] = jnp.where(low_lanes, dq_two[:rows], dq_two[rows:]).astype(
            jnp.bfloat16
        )
        for kind, grads in enumerate((dot(d_scores, q_two, 0, 0), dot(rounded, g_two, 0, 0))):
            first, second = grads[:rows], grads[2 * rows : 3 * rows]
            own_grad[pair, kind] = grads[rows : 2 * rows].astype(jnp.bfloat16)
            for slot, (chosen, term) in enumerate(
                ((lower2, second), (lower, first), (upper, second), (upper2, first))
            ):
                grad_out[pair, slot, kind] = jnp.where(chosen, term, zero_grad).astype(jnp.bfloat16)
            ctrl_out[pair, :, kind] = (
                grads[3 * rows :].astype(jnp.bfloat16).reshape(count, ctrl_rows, LANES)
            )
        for step in range(1, count):
            sum_copy(pair, step).start()
        for slot, distance in enumerate(SLOTS):
            @pl.when(inside(me + distance))
            def _():
                grad_copy(pair, slot).start()
        return 0

    lax.fori_loop(0, pairs, work, 0)

    def finish(pair, _):
        ctrl_in[pair, me] = ctrl_out[pair, me]
        for step in range(1, count):
            sum_arrival(pair, step).wait_recv()
        for slot, distance in enumerate(SLOTS):
            @pl.when(inside(me - distance))
            def _():
                grad_copy(pair, slot).wait_recv()
        for kind, (key_ref, ctrl_ref) in enumerate(((dk_ref, dck_ref), (dv_ref, dcv_ref))):
            total = own_grad[pair, kind].astype(jnp.float32)
            for slot in range(len(SLOTS)):
                total += grad_in[pair, slot, kind].astype(jnp.float32)
            key_ref[:, columns(pair)] = total.astype(jnp.bfloat16)
            ctrl_total = ctrl_in[pair, 0, kind].astype(jnp.float32)
            for source in range(1, count):
                ctrl_total += ctrl_in[pair, source, kind].astype(jnp.float32)
            ctrl_ref[:, columns(pair)] = ctrl_total.astype(jnp.bfloat16)
        return 0

    lax.fori_loop(0, pairs, finish, 0)

    def drain(pair, _):
        for step in range(1, count):
            ctrl_copy(pair, step).wait_send()
            sum_copy(pair, step).wait_send()
        for slot, distance in enumerate(SLOTS):
            @pl.when(inside(me - distance))
            def _():
                kv_copy(pair, slot).wait_send()

            @pl.when(inside(me + distance))
            def _():
                grad_copy(pair, slot).wait_send()
        return 0

    lax.fori_loop(0, pairs, drain, 0)


def fused_shards(
    query_states, key_states, value_states, d_attended, ctrl_key, ctrl_value,
    ctrl_bias, tube_lengths, tube_owner, ctrl_owner,
):
    count = lax.axis_size("seq")
    rows, width = query_states.shape
    ctrl_rows = ctrl_key.shape[0]
    pairs = width // LANES
    tube_index, owner_index = tube_tables(tube_lengths, tube_owner, count)
    position = lax.axis_index("seq")
    mine = tube_index[position]

    def member(distance):
        block = position + distance
        return (block >= 0) & (block < count) & (tube_index[jnp.clip(block, 0, count - 1)] == mine)

    flags = jnp.stack([member(distance) for distance in SLOTS])
    blocks_open = jnp.stack([flags[1] | flags[3], True, flags[2] | flags[0]])
    tube_bias = jnp.where(jnp.repeat(blocks_open, rows), 0.0, MASKED)
    heads = ctrl_bias.shape[0]
    ctrl_part = jnp.where(
        (ctrl_owner == owner_index[position])[None, :], ctrl_bias[:, None], MASKED
    )
    bias = jnp.concatenate(
        [jnp.broadcast_to(tube_bias[None, :], (heads, 3 * rows)), ctrl_part], axis=1
    ).reshape(pairs, 2, -1)
    vmem = pl.BlockSpec(memory_space=pltpu.VMEM)
    block = jax.ShapeDtypeStruct((rows, width), jnp.bfloat16)
    ctrl_block = jax.ShapeDtypeStruct((ctrl_rows, width), jnp.bfloat16)
    tile = (2, rows, LANES)
    ctrl_tile = (count, 2, ctrl_rows, LANES)
    slots = len(SLOTS)
    return pl.pallas_call(
        partial(tube_kernel, count),
        out_shape=(block, block, block, block, ctrl_block, ctrl_block),
        in_specs=[vmem] * 7 + [pl.BlockSpec(memory_space=pltpu.SMEM)],
        out_specs=[vmem] * 6,
        scratch_shapes=[
            pltpu.VMEM((pairs,) + tile, jnp.bfloat16),
            pltpu.VMEM((pairs, slots) + tile, jnp.bfloat16),
            pltpu.VMEM((pairs,) + ctrl_tile, jnp.bfloat16),
            pltpu.VMEM((pairs,) + tile, jnp.bfloat16),
            pltpu.VMEM((pairs, slots) + tile, jnp.bfloat16),
            pltpu.VMEM((pairs, slots) + tile, jnp.bfloat16),
            pltpu.VMEM((pairs,) + ctrl_tile, jnp.bfloat16),
            pltpu.VMEM((pairs,) + ctrl_tile, jnp.bfloat16),
            pltpu.SemaphoreType.DMA((pairs, slots)),
            pltpu.SemaphoreType.DMA((pairs, slots)),
            pltpu.SemaphoreType.DMA((pairs, count)),
            pltpu.SemaphoreType.DMA((pairs, count)),
            pltpu.SemaphoreType.DMA((pairs, slots)),
            pltpu.SemaphoreType.DMA((pairs, slots)),
            pltpu.SemaphoreType.DMA((pairs, count)),
            pltpu.SemaphoreType.DMA((pairs, count)),
        ],
        compiler_params=pltpu.CompilerParams(
            collective_id=0, has_side_effects=True, vmem_limit_bytes=48 * 1024 * 1024
        ),
    )(
        query_states, key_states, value_states, d_attended, ctrl_key, ctrl_value,
        bias, flags.astype(jnp.int32),
    )


def fused_or_plain(*arrays):
    tile_rows = 16
    fits = arrays[4].shape[0] % tile_rows == 0 and arrays[0].shape[0] == BLK
    return (fused_shards if fits else shards)(*arrays)


def solution(mesh):
    return jax.shard_map(
        fused_or_plain,
        mesh=mesh,
        in_specs=(
            P(("groups", "seq"), "head"),
            P(("groups", "seq"), "head"),
            P(("groups", "seq"), "head"),
            P(("groups", "seq"), "head"),
            P(("groups", "seq"), "head"),
            P(("groups", "seq"), "head"),
            P("head"),
            P("groups"),
            P("groups"),
            P("groups"),
        ),
        out_specs=(
            P(("groups", "seq"), "head"),
            P(("groups", "seq"), "head"),
            P(("groups", "seq"), "head"),
            P(("groups", "seq"), "head"),
            P(("groups", "seq"), "head"),
            P(("groups", "seq"), "head"),
        ),
        check_vma=False,
    )
```

```python
from functools import partial

import jax
import jax.numpy as jnp
from jax import lax
from jax.experimental import pallas as pl
from jax.experimental.pallas import tpu as pltpu
from jax.sharding import PartitionSpec as P

BLK = 128
REACH = 2


MASKED = -1e30


def passed_along(block, axis, distance):
    devices = range(lax.axis_size(axis))
    route = [(i - distance, i) for i in devices if i - distance in devices]
    return lax.ppermute(block, axis, route)


def tube_tables(tube_lengths, tube_owner, blocks_all):
    tube_ends = jnp.cumsum(tube_lengths, dtype=jnp.int32)
    blocks = jnp.arange(blocks_all, dtype=jnp.int32)
    tube_index = jnp.sum(
        (tube_ends[None, :] <= blocks[:, None]).astype(jnp.int32), axis=1, dtype=jnp.int32
    )
    tube_ids = jnp.arange(tube_lengths.shape[0], dtype=jnp.int32)
    matches = tube_ids[None, :] == tube_index[:, None]
    owner_index = jnp.sum(jnp.where(matches, tube_owner[None, :], 0), axis=1, dtype=jnp.int32)
    return (tube_index, owner_index)


def split_heads(rows_in, head_width):
    return rows_in.reshape(rows_in.shape[0], rows_in.shape[1] // head_width, head_width)


def scores_of(q_blk, k_blk):
    return jnp.einsum(
        "qhd,khd->hqk", q_blk, k_blk, preferred_element_type=jnp.float32
    ) * q_blk.shape[-1] ** (-0.5)


def weights_of(scores, row_high, row_total):
    return jnp.exp(scores - row_high[..., None]) / row_total[..., None]


def raise_stats(statistics, scores):
    row_high, row_total = statistics
    new_high = jnp.maximum(row_high, jnp.max(scores, axis=-1))
    row_total = row_total * jnp.exp(row_high - new_high) + jnp.sum(
        jnp.exp(scores - new_high[..., None]), axis=-1
    )
    return (new_high, row_total)


def unchanged(carried):
    return carried


def round_trip(values):
    return lax.optimization_barrier(values.astype(jnp.bfloat16)).astype(jnp.float32)


def shards(
    query_states,
    key_states,
    value_states,
    d_attended,
    ctrl_key,
    ctrl_value,
    ctrl_bias,
    tube_lengths,
    tube_owner,
    ctrl_owner,
):
    row_count, width_all = query_states.shape
    head_width = width_all // ctrl_bias.shape[0]
    head_scale = head_width ** (-0.5)
    per_device = row_count // BLK
    blocks_all = lax.axis_size("seq") * per_device
    position = lax.axis_index("seq")
    slot_count = 2 * REACH + 1
    tube_index, owner_index = tube_tables(tube_lengths, tube_owner, blocks_all)
    ctrl_pair = lax.all_gather(jnp.stack([ctrl_key, ctrl_value]), "seq", axis=1, tiled=True)
    ctrl_keys = split_heads(ctrl_pair[0], head_width)
    ctrl_values = split_heads(ctrl_pair[1], head_width)
    ctrl_shift = ctrl_bias[:, None, None]
    key_value = jnp.stack([key_states, value_states])
    lower_side = [passed_along(key_value, "seq", distance) for distance in range(REACH, 0, -1)]
    upper_side = [passed_along(key_value, "seq", -distance) for distance in range(1, REACH + 1)]
    kv_window = lower_side + [key_value] + upper_side

    def member(slot_index, block_local, tube_id):
        block_id = (position - REACH + slot_index) * per_device + block_local
        clipped = jnp.clip(block_id, 0, blocks_all - 1)
        return (block_id >= 0) & (block_id < blocks_all) & (tube_index[clipped] == tube_id)

    def window_block(window, slot_index, block_local, member_index):
        return split_heads(
            window[slot_index][member_index, block_local * BLK : (block_local + 1) * BLK],
            head_width,
        )

    def visit_keys(update, carried, tube_id, skipped):
        for slot_index in range(slot_count):
            for key_local in range(per_device):
                if slot_index == REACH and key_local == skipped:
                    continue
                carried = lax.cond(
                    member(slot_index, key_local, tube_id),
                    partial(update, slot_index=slot_index, key_local=key_local),
                    unchanged,
                    carried,
                )
        return carried

    q_blocks, g_blocks, query_tubes, ctrl_masks = ([], [], [], [])
    query_local = 0
    q_blocks.append(split_heads(query_states, head_width))
    g_blocks.append(split_heads(d_attended, head_width))
    block_id = position * per_device + query_local
    query_tubes.append(tube_index[block_id])
    ctrl_masks.append((ctrl_owner == owner_index[block_id])[None, None, :])

    def ctrl_scores(query_local):
        return jnp.where(
            ctrl_masks[query_local],
            scores_of(q_blocks[query_local], ctrl_keys) + ctrl_shift,
            MASKED,
        )

    highs, totals, deltas, attended_blocks = ([], [], [], [])
    query_local = 0
    q_blk = q_blocks[query_local]
    own_scores = scores_of(q_blk, window_block(kv_window, REACH, query_local, 0))
    row_high = jnp.max(own_scores, axis=-1)
    statistics = (row_high, jnp.sum(jnp.exp(own_scores - row_high[..., None]), axis=-1))
    statistics = raise_stats(statistics, ctrl_scores(query_local))

    def add_stats(carried, slot_index, key_local, q_blk=q_blk):
        return raise_stats(
            carried, scores_of(q_blk, window_block(kv_window, slot_index, key_local, 0))
        )

    row_high, row_total = visit_keys(add_stats, statistics, query_tubes[query_local], query_local)
    ctrl_weights = weights_of(ctrl_scores(query_local), row_high, row_total).astype(jnp.bfloat16)
    summed = jnp.einsum(
        "hqk,khd->qhd", ctrl_weights, ctrl_values, preferred_element_type=jnp.float32
    )

    def add_values(
        carried, slot_index, key_local, q_blk=q_blk, row_high=row_high, row_total=row_total
    ):
        k_blk = window_block(kv_window, slot_index, key_local, 0)
        v_blk = window_block(kv_window, slot_index, key_local, 1)
        weights = weights_of(scores_of(q_blk, k_blk), row_high, row_total).astype(jnp.bfloat16)
        return carried + jnp.einsum(
            "hqk,khd->qhd", weights, v_blk, preferred_element_type=jnp.float32
        )

    summed = visit_keys(add_values, summed, query_tubes[query_local], -1)
    attended_blk = summed.astype(jnp.bfloat16)
    row_delta = jnp.sum(
        g_blocks[query_local].astype(jnp.float32) * attended_blk.astype(jnp.float32), axis=-1
    ).T
    highs.append(row_high)
    totals.append(row_total)
    deltas.append(row_delta)
    attended_blocks.append(attended_blk)

    def grad_terms(query_local, v_blk, scores):
        weights = weights_of(scores, highs[query_local], totals[query_local])
        d_prob = jnp.einsum(
            "qhd,khd->hqk", g_blocks[query_local], v_blk, preferred_element_type=jnp.float32
        )
        d_scores = (weights * (d_prob - deltas[query_local][..., None])).astype(jnp.bfloat16)
        return (weights.astype(jnp.bfloat16), d_scores)

    query_local = 0
    rounded, d_scores = grad_terms(query_local, ctrl_values, ctrl_scores(query_local))
    d_queries = [
        jnp.einsum("hqk,khd->qhd", d_scores, ctrl_keys, preferred_element_type=jnp.float32)
        * head_scale
    ]
    ctrl_key_grad = (
        jnp.einsum(
            "hqk,qhd->khd", d_scores, q_blocks[query_local], preferred_element_type=jnp.float32
        )
        * head_scale
    )
    ctrl_value_grad = jnp.einsum(
        "hqk,qhd->khd", rounded, g_blocks[query_local], preferred_element_type=jnp.float32
    )
    block_zeros = jnp.zeros((BLK, width_all // head_width, head_width), jnp.float32)
    key_parts = jnp.zeros((2, row_count, width_all), jnp.float32)
    for slot_index in range(slot_count):
        key_local = 0
        k_blk = window_block(kv_window, slot_index, key_local, 0)
        v_blk = window_block(kv_window, slot_index, key_local, 1)
        key_grad = block_zeros
        value_grad = block_zeros
        query_local = 0

        def add_grads(carried, query_local=query_local, k_blk=k_blk, v_blk=v_blk):
            rounded, d_scores = grad_terms(
                query_local, v_blk, scores_of(q_blocks[query_local], k_blk)
            )
            d_query_blk = (
                carried[0]
                + jnp.einsum("hqk,khd->qhd", d_scores, k_blk, preferred_element_type=jnp.float32)
                * head_scale
            )
            key_term = (
                jnp.einsum(
                    "hqk,qhd->khd",
                    d_scores,
                    q_blocks[query_local],
                    preferred_element_type=jnp.float32,
                )
                * head_scale
            )
            value_term = jnp.einsum(
                "hqk,qhd->khd", rounded, g_blocks[query_local], preferred_element_type=jnp.float32
            )
            return (d_query_blk, key_term, value_term)

        carried = lax.cond(
            member(slot_index, key_local, query_tubes[query_local]),
            add_grads,
            unchanged,
            (d_queries[query_local], key_grad, value_grad),
        )
        d_queries[query_local], key_grad, value_grad = carried
        slot_pieces = jnp.stack([key_grad, value_grad]).reshape(2, BLK, width_all)
        if slot_index == REACH:
            key_parts = key_parts + round_trip(slot_pieces)
        else:
            received = passed_along(slot_pieces.astype(jnp.bfloat16), "seq", slot_index - REACH)
            key_parts = key_parts + received.astype(jnp.float32)
    key_results = key_parts.astype(jnp.bfloat16)
    ctrl_terms = jnp.stack(
        [ctrl_key_grad.reshape(-1, width_all), ctrl_value_grad.reshape(-1, width_all)]
    )
    ctrl_results = lax.psum_scatter(ctrl_terms, "seq", scatter_dimension=1, tiled=True).astype(
        jnp.bfloat16
    )
    attended = attended_blocks[0].reshape(row_count, width_all)
    d_query = d_queries[0].reshape(row_count, width_all).astype(jnp.bfloat16)
    return (attended, d_query, key_results[0], key_results[1], ctrl_results[0], ctrl_results[1])


MESH = pl.DeviceIdType.MESH
SLOTS = (-2, -1, 1, 2)
LANES = 128
AHEAD = 2


def masked_pair(rows, low_lanes, factor):
    first = low_lanes.astype(jnp.float32) * factor
    second = factor - first
    return jnp.concatenate(
        [rows * first.astype(rows.dtype), rows * second.astype(rows.dtype)], axis=0
    )


def dot(left, right, left_dim, right_dim):
    return lax.dot_general(
        left, right, (((left_dim,), (right_dim,)), ((), ())), preferred_element_type=jnp.float32
    )


def tube_kernel(
    count, q_hbm, k_hbm, v_hbm, g_hbm, ck_hbm, cv_hbm,
    bias_hbm, length_hbm, owner_hbm, tag_hbm,
    att_ref, dq_ref, dk_ref, dv_ref, dck_ref, dcv_ref,
    q_ref, g_ref, own, window, ctrl, own_grad, grad_out, grad_in, ctrl_out, ctrl_mid, ctrl_in,
    bias_ref, length_ref, owner_ref, tag_ref, load_sem, query_sem,
    kv_send, kv_recv, ctrl_send, ctrl_recv, grad_send, grad_recv,
    mid_send, mid_recv, sum_send, sum_recv,
):
    me = lax.axis_index("seq")
    column = lax.rem(me, 2)
    peer = me + 1 - 2 * column
    level = me // 2
    levels = count // 2
    rows = q_ref.shape[0]
    ctrl_rows = ck_hbm.shape[0]
    pairs = q_ref.shape[1] // LANES
    low_lanes = lax.broadcasted_iota(jnp.int32, (1, LANES), 1) < LANES // 2

    def inside(device):
        return (device >= 0) & (device < count)

    def columns(pair):
        return pl.ds(pl.multiple_of(pair * LANES, LANES), LANES)

    def kv_copy(pair, slot):
        return pltpu.make_async_remote_copy(
            own.at[pair], window.at[pair, slot], kv_send.at[pair, slot], kv_recv.at[pair, slot],
            device_id={"seq": me - SLOTS[slot]}, device_id_type=MESH,
        )

    def grad_copy(pair, slot):
        return pltpu.make_async_remote_copy(
            grad_out.at[pair, slot], grad_in.at[pair, slot],
            grad_send.at[pair, slot], grad_recv.at[pair, slot],
            device_id={"seq": me + SLOTS[slot]}, device_id_type=MESH,
        )

    def mate(step):
        return lax.rem(me + 2 * step, count)

    def mate_before(step):
        return lax.rem(me - 2 * step + count, count)

    def ctrl_copy(pair, step):
        return pltpu.make_async_remote_copy(
            ctrl.at[pair, me], ctrl.at[pair, me], ctrl_send.at[pair, step], ctrl_recv.at[pair, step],
            device_id={"seq": mate(step) if step else peer}, device_id_type=MESH,
        )

    def ctrl_arrival(pair, step):
        source = mate_before(step) if step else peer
        return pltpu.make_async_remote_copy(
            ctrl.at[pair, source], ctrl.at[pair, source],
            ctrl_send.at[pair, step], ctrl_recv.at[pair, step],
            device_id={"seq": source}, device_id_type=MESH,
        )

    def ctrl_onward(pair, step):
        source = mate_before(step)
        return pltpu.make_async_remote_copy(
            ctrl.at[pair, source], ctrl.at[pair, source],
            ctrl_send.at[pair, levels + step], ctrl_recv.at[pair, levels + step],
            device_id={"seq": peer}, device_id_type=MESH,
        )

    def ctrl_onward_arrival(pair, step):
        source = mate_before(step) + 1 - 2 * column
        return pltpu.make_async_remote_copy(
            ctrl.at[pair, source], ctrl.at[pair, source],
            ctrl_send.at[pair, levels + step], ctrl_recv.at[pair, levels + step],
            device_id={"seq": peer}, device_id_type=MESH,
        )

    def mid_copy(pair):
        return pltpu.make_async_remote_copy(
            ctrl_out.at[pair, 1 - column], ctrl_mid.at[pair], mid_send.at[pair], mid_recv.at[pair],
            device_id={"seq": peer}, device_id_type=MESH,
        )

    def sum_copy(pair, step):
        return pltpu.make_async_remote_copy(
            ctrl_out.at[pair, column, mate(step) // 2], ctrl_in.at[pair, level],
            sum_send.at[pair, step], sum_recv.at[pair, step],
            device_id={"seq": mate(step)}, device_id_type=MESH,
        )

    def sum_arrival(pair, step):
        source = mate_before(step)
        return pltpu.make_async_remote_copy(
            ctrl_out.at[pair, column, level], ctrl_in.at[pair, source // 2],
            sum_send.at[pair, step], sum_recv.at[pair, step],
            device_id={"seq": source}, device_id_type=MESH,
        )

    def loads(pair):
        part = columns(pair)
        return [
            pltpu.make_async_copy(source.at[:, part], target, load_sem.at[pair, i])
            for i, (source, target) in enumerate((
                (ck_hbm, ctrl.at[pair, me, 0]), (cv_hbm, ctrl.at[pair, me, 1]),
                (k_hbm, own.at[pair, 0]), (v_hbm, own.at[pair, 1]),
            ))
        ]

    def query_loads():
        return (
            pltpu.make_async_copy(q_hbm, q_ref, query_sem.at[0]),
            pltpu.make_async_copy(g_hbm, g_ref, query_sem.at[1]),
            pltpu.make_async_copy(bias_hbm, bias_ref, query_sem.at[2]),
            pltpu.make_async_copy(length_hbm, length_ref, query_sem.at[3]),
            pltpu.make_async_copy(owner_hbm, owner_ref, query_sem.at[4]),
            pltpu.make_async_copy(tag_hbm, tag_ref, query_sem.at[5]),
        )

    def start_loads(pair, _):
        for copy in loads(pair):
            copy.start()
        return 0

    lax.fori_loop(0, pairs, start_loads, 0)
    for copy in query_loads():
        copy.start()
    for slot, distance in enumerate(SLOTS):
        @pl.when(jnp.logical_not(inside(me + distance)))
        def _():
            window[:, slot] = jnp.zeros((pairs,) + window.shape[2:], window.dtype)

        @pl.when(jnp.logical_not(inside(me - distance)))
        def _():
            grad_in[:, slot] = jnp.zeros((pairs,) + grad_in.shape[2:], grad_in.dtype)

    barrier = pltpu.get_barrier_semaphore()
    for step in range(1, count):
        pl.semaphore_signal(
            barrier, inc=1, device_id={"seq": lax.rem(me + step, count)}, device_id_type=MESH
        )
    pl.semaphore_wait(barrier, count - 1)

    def send(pair, _):
        for copy in loads(pair):
            copy.wait()
        for step in range(levels):
            ctrl_copy(pair, step).start()
        for slot, distance in enumerate(SLOTS):
            @pl.when(inside(me - distance))
            def _():
                kv_copy(pair, slot).start()
        return 0

    lax.fori_loop(0, pairs, send, 0)

    for copy in query_loads():
        copy.wait()
    tubes = length_ref.shape[0]
    ends = []
    for tube in range(tubes):
        ends.append(length_ref[tube] + (ends[-1] if ends else 0))

    def tube_at(block):
        return sum(jnp.where(end <= block, 1, 0) for end in ends)

    mine = tube_at(me)
    owner = sum(jnp.where(mine == tube, owner_ref[tube], 0) for tube in range(tubes))
    lower2, lower, upper, upper2 = (
        inside(me + distance) & (tube_at(me + distance) == mine) for distance in SLOTS
    )
    first_bias = jnp.full((1, rows), jnp.where(lower | upper2, 0.0, MASKED), jnp.float32)
    second_bias = jnp.full((1, rows), jnp.where(upper | lower2, 0.0, MASKED), jnp.float32)
    own_bias = jnp.zeros((1, rows), jnp.float32)
    ctrl_open = tag_ref[...].reshape(1, count * ctrl_rows) == owner

    def bias_of(head):
        ctrl_bias = jnp.where(ctrl_open, bias_ref[head], MASKED)
        return jnp.concatenate([first_bias, own_bias, second_bias, ctrl_bias], axis=1)

    zero_block = jnp.zeros((rows, LANES), jnp.bfloat16)
    zero_grad = jnp.zeros((rows, LANES), jnp.float32)

    def relay(pair):
        for step in range(1, levels):
            ctrl_arrival(pair, step).wait_recv()
            ctrl_onward(pair, step).start()

    def column_sums(pair):
        mid_copy(pair).wait()
        ctrl_out[pair, column] = (
            ctrl_out[pair, column].astype(jnp.float32) + ctrl_mid[pair].astype(jnp.float32)
        ).astype(jnp.bfloat16)
        for step in range(1, levels):
            sum_copy(pair, step).start()

    def work(pair, _):
        @pl.when(pair + AHEAD < pairs)
        def _():
            relay(pair + AHEAD)

        ctrl_arrival(pair, 0).wait_recv()
        for step in range(1, levels):
            ctrl_onward_arrival(pair, step).wait_recv()
        for slot, distance in enumerate(SLOTS):
            @pl.when(inside(me + distance))
            def _():
                kv_copy(pair, slot).wait_recv()

        def gathered(kind):
            first = jnp.where(
                lower, window[pair, 1, kind], jnp.where(upper2, window[pair, 3, kind], zero_block)
            )
            second = jnp.where(
                upper, window[pair, 2, kind], jnp.where(lower2, window[pair, 0, kind], zero_block)
            )
            shared = ctrl[pair, :, kind].reshape(count * ctrl_rows, LANES)
            return jnp.concatenate([first, own[pair, kind], second, shared], axis=0)

        keys = gathered(0)
        values = gathered(1)
        q_two = masked_pair(q_ref[:, columns(pair)], low_lanes, 0.125)
        g_two = masked_pair(g_ref[:, columns(pair)], low_lanes, 1.0)
        scores = dot(q_two, keys, 1, 1)
        scores = jnp.concatenate(
            [scores[:rows] + bias_of(2 * pair), scores[rows:] + bias_of(2 * pair + 1)], axis=0
        )
        raised = jnp.exp(scores - jnp.max(scores, axis=1, keepdims=True))
        weights = raised * (1.0 / jnp.sum(raised, axis=1, keepdims=True))
        rounded = weights.astype(jnp.bfloat16)
        out_two = dot(rounded, values, 1, 0)
        attended = jnp.where(low_lanes, out_two[:rows], out_two[rows:]).astype(jnp.bfloat16)
        att_ref[:, columns(pair)] = attended
        attended = attended.astype(jnp.float32)
        delta = jnp.sum(
            g_two.astype(jnp.float32) * jnp.concatenate([attended, attended], axis=0),
            axis=1, keepdims=True,
        )
        d_scores = (weights * (dot(g_two, values, 1, 1) - delta)).astype(jnp.bfloat16)
        dq_two = dot(d_scores, keys, 1, 0) * 0.125
        dq_ref[:, columns(pair)] = jnp.where(low_lanes, dq_two[:rows], dq_two[rows:]).astype(
            jnp.bfloat16
        )
        for kind, grads in enumerate((dot(d_scores, q_two, 0, 0), dot(rounded, g_two, 0, 0))):
            first, second = grads[:rows], grads[2 * rows : 3 * rows]
            own_grad[pair, kind] = grads[rows : 2 * rows].astype(jnp.bfloat16)
            for slot, (chosen, term) in enumerate(
                ((lower2, second), (lower, first), (upper, second), (upper2, first))
            ):
                grad_out[pair, slot, kind] = jnp.where(chosen, term, zero_grad).astype(jnp.bfloat16)
            shared = grads[3 * rows :].astype(jnp.bfloat16)
            for device in range(count):
                ctrl_out[pair, device % 2, device // 2, kind] = (
                    shared[device * ctrl_rows : (device + 1) * ctrl_rows]
                )
        mid_copy(pair).start()
        for slot, distance in enumerate(SLOTS):
            @pl.when(inside(me + distance))
            def _():
                grad_copy(pair, slot).start()

        @pl.when(pair > 0)
        def _():
            column_sums(pair - 1)

        return 0

    for pair in range(AHEAD):
        relay(pair)
    lax.fori_loop(0, pairs, work, 0)
    column_sums(pairs - 1)

    def finish(pair, _):
        ctrl_in[pair, level] = ctrl_out[pair, column, level]
        for step in range(1, levels):
            sum_arrival(pair, step).wait_recv()
        for slot, distance in enumerate(SLOTS):
            @pl.when(inside(me - distance))
            def _():
                grad_copy(pair, slot).wait_recv()
        for kind, (key_ref, ctrl_ref) in enumerate(((dk_ref, dck_ref), (dv_ref, dcv_ref))):
            total = own_grad[pair, kind].astype(jnp.float32)
            for slot in range(len(SLOTS)):
                total += grad_in[pair, slot, kind].astype(jnp.float32)
            key_ref[:, columns(pair)] = total.astype(jnp.bfloat16)
            ctrl_total = ctrl_in[pair, 0, kind].astype(jnp.float32)
            for source in range(1, levels):
                ctrl_total += ctrl_in[pair, source, kind].astype(jnp.float32)
            ctrl_ref[:, columns(pair)] = ctrl_total.astype(jnp.bfloat16)
        return 0

    lax.fori_loop(0, pairs, finish, 0)

    def drain(pair, _):
        for step in range(levels):
            ctrl_copy(pair, step).wait_send()
        for step in range(1, levels):
            ctrl_onward(pair, step).wait_send()
            sum_copy(pair, step).wait_send()
        for slot, distance in enumerate(SLOTS):
            @pl.when(inside(me - distance))
            def _():
                kv_copy(pair, slot).wait_send()

            @pl.when(inside(me + distance))
            def _():
                grad_copy(pair, slot).wait_send()
        return 0

    lax.fori_loop(0, pairs, drain, 0)


def fused_shards(
    query_states, key_states, value_states, d_attended, ctrl_key, ctrl_value,
    ctrl_bias, tube_lengths, tube_owner, ctrl_owner,
):
    count = lax.axis_size("seq")
    rows, width = query_states.shape
    ctrl_rows = ctrl_key.shape[0]
    pairs = width // LANES
    vmem = pl.BlockSpec(memory_space=pltpu.VMEM)
    hbm = pl.BlockSpec(memory_space=pl.ANY)
    block = jax.ShapeDtypeStruct((rows, width), jnp.bfloat16)
    ctrl_block = jax.ShapeDtypeStruct((ctrl_rows, width), jnp.bfloat16)
    tile = (2, rows, LANES)
    ctrl_tile = (2, ctrl_rows, LANES)
    slots = len(SLOTS)
    results = pl.pallas_call(
        partial(tube_kernel, count),
        out_shape=(block, block, block, block, ctrl_block, ctrl_block),
        in_specs=[pl.BlockSpec(memory_space=pltpu.HBM)] * 10,
        out_specs=[vmem] * 6,
        scratch_shapes=[
            pltpu.VMEM((rows, width), jnp.bfloat16),
            pltpu.VMEM((rows, width), jnp.bfloat16),
            pltpu.VMEM((pairs,) + tile, jnp.bfloat16),
            pltpu.VMEM((pairs, slots) + tile, jnp.bfloat16),
            pltpu.VMEM((pairs, count) + ctrl_tile, jnp.bfloat16),
            pltpu.VMEM((pairs,) + tile, jnp.bfloat16),
            pltpu.VMEM((pairs, slots) + tile, jnp.bfloat16),
            pltpu.VMEM((pairs, slots) + tile, jnp.bfloat16),
            pltpu.VMEM((pairs, 2, count // 2) + ctrl_tile, jnp.bfloat16),
            pltpu.VMEM((pairs, count // 2) + ctrl_tile, jnp.bfloat16),
            pltpu.VMEM((pairs, count // 2) + ctrl_tile, jnp.bfloat16),
            pltpu.SMEM(ctrl_bias.shape, jnp.float32),
            pltpu.SMEM(tube_lengths.shape, jnp.int32),
            pltpu.SMEM(tube_owner.shape, jnp.int32),
            pltpu.VMEM(ctrl_owner.shape, jnp.int32),
            pltpu.SemaphoreType.DMA((pairs, 4)),
            pltpu.SemaphoreType.DMA((6,)),
            pltpu.SemaphoreType.DMA((pairs, slots)),
            pltpu.SemaphoreType.DMA((pairs, slots)),
            pltpu.SemaphoreType.DMA((pairs, count)),
            pltpu.SemaphoreType.DMA((pairs, count)),
            pltpu.SemaphoreType.DMA((pairs, slots)),
            pltpu.SemaphoreType.DMA((pairs, slots)),
            pltpu.SemaphoreType.DMA((pairs,)),
            pltpu.SemaphoreType.DMA((pairs,)),
            pltpu.SemaphoreType.DMA((pairs, count // 2)),
            pltpu.SemaphoreType.DMA((pairs, count // 2)),
        ],
        compiler_params=pltpu.CompilerParams(
            collective_id=0, has_side_effects=True, vmem_limit_bytes=64 * 1024 * 1024 - 65536
        ),
    )(
        query_states, key_states, value_states, d_attended, ctrl_key, ctrl_value,
        ctrl_bias, tube_lengths, tube_owner, ctrl_owner,
    )
    return pl.pallas_call(
        hand_over,
        out_shape=(block, block, block, block, ctrl_block, ctrl_block),
        in_specs=[hbm] * 6,
        out_specs=[hbm] * 6,
        scratch_shapes=[pltpu.SemaphoreType.DMA((6,))],
        compiler_params=pltpu.CompilerParams(vmem_limit_bytes=64 * 1024 * 1024 - 65536),
    )(*results)


def hand_over(*refs):
    sems = refs[-1]
    copies = [
        pltpu.make_async_copy(refs[i], refs[6 + i], sems.at[i]) for i in range(6)
    ]
    for copy in copies:
        copy.start()
    for copy in copies:
        copy.wait()


def fused_or_plain(*arrays):
    tile_rows = 16
    fits = arrays[4].shape[0] % tile_rows == 0 and arrays[0].shape[0] == BLK
    return (fused_shards if fits else shards)(*arrays)


def solution(mesh):
    return jax.shard_map(
        fused_or_plain,
        mesh=mesh,
        in_specs=(
            P(("groups", "seq"), "head"),
            P(("groups", "seq"), "head"),
            P(("groups", "seq"), "head"),
            P(("groups", "seq"), "head"),
            P(("groups", "seq"), "head"),
            P(("groups", "seq"), "head"),
            P("head"),
            P("groups"),
            P("groups"),
            P("groups"),
        ),
        out_specs=(
            P(("groups", "seq"), "head"),
            P(("groups", "seq"), "head"),
            P(("groups", "seq"), "head"),
            P(("groups", "seq"), "head"),
            P(("groups", "seq"), "head"),
            P(("groups", "seq"), "head"),
        ),
        check_vma=False,
    )
```

```python
from functools import partial

import jax
import jax.numpy as jnp
from jax import lax
from jax.experimental import pallas as pl
from jax.experimental.pallas import tpu as pltpu
from jax.sharding import PartitionSpec as P

BLK = 128
REACH = 2


MASKED = -1e30


def passed_along(block, axis, distance):
    devices = range(lax.axis_size(axis))
    route = [(i - distance, i) for i in devices if i - distance in devices]
    return lax.ppermute(block, axis, route)


def tube_tables(tube_lengths, tube_owner, blocks_all):
    tube_ends = jnp.cumsum(tube_lengths, dtype=jnp.int32)
    blocks = jnp.arange(blocks_all, dtype=jnp.int32)
    tube_index = jnp.sum(
        (tube_ends[None, :] <= blocks[:, None]).astype(jnp.int32), axis=1, dtype=jnp.int32
    )
    tube_ids = jnp.arange(tube_lengths.shape[0], dtype=jnp.int32)
    matches = tube_ids[None, :] == tube_index[:, None]
    owner_index = jnp.sum(jnp.where(matches, tube_owner[None, :], 0), axis=1, dtype=jnp.int32)
    return (tube_index, owner_index)


def split_heads(rows_in, head_width):
    return rows_in.reshape(rows_in.shape[0], rows_in.shape[1] // head_width, head_width)


def scores_of(q_blk, k_blk):
    return jnp.einsum(
        "qhd,khd->hqk", q_blk, k_blk, preferred_element_type=jnp.float32
    ) * q_blk.shape[-1] ** (-0.5)


def weights_of(scores, row_high, row_total):
    return jnp.exp(scores - row_high[..., None]) / row_total[..., None]


def raise_stats(statistics, scores):
    row_high, row_total = statistics
    new_high = jnp.maximum(row_high, jnp.max(scores, axis=-1))
    row_total = row_total * jnp.exp(row_high - new_high) + jnp.sum(
        jnp.exp(scores - new_high[..., None]), axis=-1
    )
    return (new_high, row_total)


def unchanged(carried):
    return carried


def round_trip(values):
    return lax.optimization_barrier(values.astype(jnp.bfloat16)).astype(jnp.float32)


def shards(
    query_states,
    key_states,
    value_states,
    d_attended,
    ctrl_key,
    ctrl_value,
    ctrl_bias,
    tube_lengths,
    tube_owner,
    ctrl_owner,
):
    row_count, width_all = query_states.shape
    head_width = width_all // ctrl_bias.shape[0]
    head_scale = head_width ** (-0.5)
    per_device = row_count // BLK
    blocks_all = lax.axis_size("seq") * per_device
    position = lax.axis_index("seq")
    slot_count = 2 * REACH + 1
    tube_index, owner_index = tube_tables(tube_lengths, tube_owner, blocks_all)
    ctrl_pair = lax.all_gather(jnp.stack([ctrl_key, ctrl_value]), "seq", axis=1, tiled=True)
    ctrl_keys = split_heads(ctrl_pair[0], head_width)
    ctrl_values = split_heads(ctrl_pair[1], head_width)
    ctrl_shift = ctrl_bias[:, None, None]
    key_value = jnp.stack([key_states, value_states])
    lower_side = [passed_along(key_value, "seq", distance) for distance in range(REACH, 0, -1)]
    upper_side = [passed_along(key_value, "seq", -distance) for distance in range(1, REACH + 1)]
    kv_window = lower_side + [key_value] + upper_side

    def member(slot_index, block_local, tube_id):
        block_id = (position - REACH + slot_index) * per_device + block_local
        clipped = jnp.clip(block_id, 0, blocks_all - 1)
        return (block_id >= 0) & (block_id < blocks_all) & (tube_index[clipped] == tube_id)

    def window_block(window, slot_index, block_local, member_index):
        return split_heads(
            window[slot_index][member_index, block_local * BLK : (block_local + 1) * BLK],
            head_width,
        )

    def visit_keys(update, carried, tube_id, skipped):
        for slot_index in range(slot_count):
            for key_local in range(per_device):
                if slot_index == REACH and key_local == skipped:
                    continue
                carried = lax.cond(
                    member(slot_index, key_local, tube_id),
                    partial(update, slot_index=slot_index, key_local=key_local),
                    unchanged,
                    carried,
                )
        return carried

    q_blocks, g_blocks, query_tubes, ctrl_masks = ([], [], [], [])
    query_local = 0
    q_blocks.append(split_heads(query_states, head_width))
    g_blocks.append(split_heads(d_attended, head_width))
    block_id = position * per_device + query_local
    query_tubes.append(tube_index[block_id])
    ctrl_masks.append((ctrl_owner == owner_index[block_id])[None, None, :])

    def ctrl_scores(query_local):
        return jnp.where(
            ctrl_masks[query_local],
            scores_of(q_blocks[query_local], ctrl_keys) + ctrl_shift,
            MASKED,
        )

    highs, totals, deltas, attended_blocks = ([], [], [], [])
    query_local = 0
    q_blk = q_blocks[query_local]
    own_scores = scores_of(q_blk, window_block(kv_window, REACH, query_local, 0))
    row_high = jnp.max(own_scores, axis=-1)
    statistics = (row_high, jnp.sum(jnp.exp(own_scores - row_high[..., None]), axis=-1))
    statistics = raise_stats(statistics, ctrl_scores(query_local))

    def add_stats(carried, slot_index, key_local, q_blk=q_blk):
        return raise_stats(
            carried, scores_of(q_blk, window_block(kv_window, slot_index, key_local, 0))
        )

    row_high, row_total = visit_keys(add_stats, statistics, query_tubes[query_local], query_local)
    ctrl_weights = weights_of(ctrl_scores(query_local), row_high, row_total).astype(jnp.bfloat16)
    summed = jnp.einsum(
        "hqk,khd->qhd", ctrl_weights, ctrl_values, preferred_element_type=jnp.float32
    )

    def add_values(
        carried, slot_index, key_local, q_blk=q_blk, row_high=row_high, row_total=row_total
    ):
        k_blk = window_block(kv_window, slot_index, key_local, 0)
        v_blk = window_block(kv_window, slot_index, key_local, 1)
        weights = weights_of(scores_of(q_blk, k_blk), row_high, row_total).astype(jnp.bfloat16)
        return carried + jnp.einsum(
            "hqk,khd->qhd", weights, v_blk, preferred_element_type=jnp.float32
        )

    summed = visit_keys(add_values, summed, query_tubes[query_local], -1)
    attended_blk = summed.astype(jnp.bfloat16)
    row_delta = jnp.sum(
        g_blocks[query_local].astype(jnp.float32) * attended_blk.astype(jnp.float32), axis=-1
    ).T
    highs.append(row_high)
    totals.append(row_total)
    deltas.append(row_delta)
    attended_blocks.append(attended_blk)

    def grad_terms(query_local, v_blk, scores):
        weights = weights_of(scores, highs[query_local], totals[query_local])
        d_prob = jnp.einsum(
            "qhd,khd->hqk", g_blocks[query_local], v_blk, preferred_element_type=jnp.float32
        )
        d_scores = (weights * (d_prob - deltas[query_local][..., None])).astype(jnp.bfloat16)
        return (weights.astype(jnp.bfloat16), d_scores)

    query_local = 0
    rounded, d_scores = grad_terms(query_local, ctrl_values, ctrl_scores(query_local))
    d_queries = [
        jnp.einsum("hqk,khd->qhd", d_scores, ctrl_keys, preferred_element_type=jnp.float32)
        * head_scale
    ]
    ctrl_key_grad = (
        jnp.einsum(
            "hqk,qhd->khd", d_scores, q_blocks[query_local], preferred_element_type=jnp.float32
        )
        * head_scale
    )
    ctrl_value_grad = jnp.einsum(
        "hqk,qhd->khd", rounded, g_blocks[query_local], preferred_element_type=jnp.float32
    )
    block_zeros = jnp.zeros((BLK, width_all // head_width, head_width), jnp.float32)
    key_parts = jnp.zeros((2, row_count, width_all), jnp.float32)
    for slot_index in range(slot_count):
        key_local = 0
        k_blk = window_block(kv_window, slot_index, key_local, 0)
        v_blk = window_block(kv_window, slot_index, key_local, 1)
        key_grad = block_zeros
        value_grad = block_zeros
        query_local = 0

        def add_grads(carried, query_local=query_local, k_blk=k_blk, v_blk=v_blk):
            rounded, d_scores = grad_terms(
                query_local, v_blk, scores_of(q_blocks[query_local], k_blk)
            )
            d_query_blk = (
                carried[0]
                + jnp.einsum("hqk,khd->qhd", d_scores, k_blk, preferred_element_type=jnp.float32)
                * head_scale
            )
            key_term = (
                jnp.einsum(
                    "hqk,qhd->khd",
                    d_scores,
                    q_blocks[query_local],
                    preferred_element_type=jnp.float32,
                )
                * head_scale
            )
            value_term = jnp.einsum(
                "hqk,qhd->khd", rounded, g_blocks[query_local], preferred_element_type=jnp.float32
            )
            return (d_query_blk, key_term, value_term)

        carried = lax.cond(
            member(slot_index, key_local, query_tubes[query_local]),
            add_grads,
            unchanged,
            (d_queries[query_local], key_grad, value_grad),
        )
        d_queries[query_local], key_grad, value_grad = carried
        slot_pieces = jnp.stack([key_grad, value_grad]).reshape(2, BLK, width_all)
        if slot_index == REACH:
            key_parts = key_parts + round_trip(slot_pieces)
        else:
            received = passed_along(slot_pieces.astype(jnp.bfloat16), "seq", slot_index - REACH)
            key_parts = key_parts + received.astype(jnp.float32)
    key_results = key_parts.astype(jnp.bfloat16)
    ctrl_terms = jnp.stack(
        [ctrl_key_grad.reshape(-1, width_all), ctrl_value_grad.reshape(-1, width_all)]
    )
    ctrl_results = lax.psum_scatter(ctrl_terms, "seq", scatter_dimension=1, tiled=True).astype(
        jnp.bfloat16
    )
    attended = attended_blocks[0].reshape(row_count, width_all)
    d_query = d_queries[0].reshape(row_count, width_all).astype(jnp.bfloat16)
    return (attended, d_query, key_results[0], key_results[1], ctrl_results[0], ctrl_results[1])


MESH = pl.DeviceIdType.MESH
SLOTS = (-2, -1, 1, 2)
LANES = 128
AHEAD = 2


def masked_pair(rows, low_lanes, factor):
    first = low_lanes.astype(jnp.float32) * factor
    second = factor - first
    return jnp.concatenate(
        [rows * first.astype(rows.dtype), rows * second.astype(rows.dtype)], axis=0
    )


def dot(left, right, left_dim, right_dim):
    return lax.dot_general(
        left, right, (((left_dim,), (right_dim,)), ((), ())), preferred_element_type=jnp.float32
    )


def tube_kernel(
    count, q_hbm, k_hbm, v_hbm, g_hbm, ck_hbm, cv_hbm,
    bias_hbm, length_hbm, owner_hbm, tag_hbm,
    att_ref, dq_ref, dk_ref, dv_ref, dck_ref, dcv_ref,
    q_ref, g_ref, own, window, ctrl, own_grad, grad_out, grad_in, ctrl_out, ctrl_mid, ctrl_in,
    bias_ref, length_ref, owner_ref, tag_ref, load_sem, query_sem,
    kv_send, kv_recv, ctrl_send, ctrl_recv, grad_send, grad_recv,
    mid_send, mid_recv, sum_send, sum_recv,
):
    me = lax.axis_index("seq")
    column = lax.rem(me, 2)
    peer = me + 1 - 2 * column
    level = me // 2
    levels = count // 2
    rows = q_ref.shape[0]
    ctrl_rows = ck_hbm.shape[0]
    pairs = q_ref.shape[1] // LANES
    low_lanes = lax.broadcasted_iota(jnp.int32, (1, LANES), 1) < LANES // 2

    def inside(device):
        return (device >= 0) & (device < count)

    def columns(pair):
        return pl.ds(pl.multiple_of(pair * LANES, LANES), LANES)

    def kv_copy(pair, slot):
        return pltpu.make_async_remote_copy(
            own.at[pair], window.at[pair, slot], kv_send.at[pair, slot], kv_recv.at[pair, slot],
            device_id={"seq": me - SLOTS[slot]}, device_id_type=MESH,
        )

    def grad_copy(pair, slot):
        return pltpu.make_async_remote_copy(
            grad_out.at[pair, slot], grad_in.at[pair, slot],
            grad_send.at[pair, slot], grad_recv.at[pair, slot],
            device_id={"seq": me + SLOTS[slot]}, device_id_type=MESH,
        )

    def mate(step):
        return lax.rem(me + 2 * step, count)

    def mate_before(step):
        return lax.rem(me - 2 * step + count, count)

    def ctrl_copy(pair, step):
        return pltpu.make_async_remote_copy(
            ctrl.at[pair, me], ctrl.at[pair, me], ctrl_send.at[pair, step], ctrl_recv.at[pair, step],
            device_id={"seq": mate(step) if step else peer}, device_id_type=MESH,
        )

    def ctrl_arrival(pair, step):
        source = mate_before(step) if step else peer
        return pltpu.make_async_remote_copy(
            ctrl.at[pair, source], ctrl.at[pair, source],
            ctrl_send.at[pair, step], ctrl_recv.at[pair, step],
            device_id={"seq": source}, device_id_type=MESH,
        )

    def ctrl_onward(pair, step):
        source = mate_before(step)
        return pltpu.make_async_remote_copy(
            ctrl.at[pair, source], ctrl.at[pair, source],
            ctrl_send.at[pair, levels + step], ctrl_recv.at[pair, levels + step],
            device_id={"seq": peer}, device_id_type=MESH,
        )

    def ctrl_onward_arrival(pair, step):
        source = mate_before(step) + 1 - 2 * column
        return pltpu.make_async_remote_copy(
            ctrl.at[pair, source], ctrl.at[pair, source],
            ctrl_send.at[pair, levels + step], ctrl_recv.at[pair, levels + step],
            device_id={"seq": peer}, device_id_type=MESH,
        )

    def mid_copy(pair):
        return pltpu.make_async_remote_copy(
            ctrl_out.at[pair, 1 - column], ctrl_mid.at[pair], mid_send.at[pair], mid_recv.at[pair],
            device_id={"seq": peer}, device_id_type=MESH,
        )

    def sum_copy(pair, step):
        return pltpu.make_async_remote_copy(
            ctrl_out.at[pair, column, mate(step) // 2], ctrl_in.at[pair, level],
            sum_send.at[pair, step], sum_recv.at[pair, step],
            device_id={"seq": mate(step)}, device_id_type=MESH,
        )

    def sum_arrival(pair, step):
        source = mate_before(step)
        return pltpu.make_async_remote_copy(
            ctrl_out.at[pair, column, level], ctrl_in.at[pair, source // 2],
            sum_send.at[pair, step], sum_recv.at[pair, step],
            device_id={"seq": source}, device_id_type=MESH,
        )

    def loads(pair):
        part = columns(pair)
        return [
            pltpu.make_async_copy(source.at[:, part], target, load_sem.at[pair, i])
            for i, (source, target) in enumerate((
                (ck_hbm, ctrl.at[pair, me, 0]), (cv_hbm, ctrl.at[pair, me, 1]),
                (k_hbm, own.at[pair, 0]), (v_hbm, own.at[pair, 1]),
            ))
        ]

    def query_loads():
        return (
            pltpu.make_async_copy(q_hbm, q_ref, query_sem.at[0]),
            pltpu.make_async_copy(g_hbm, g_ref, query_sem.at[1]),
            pltpu.make_async_copy(bias_hbm, bias_ref, query_sem.at[2]),
            pltpu.make_async_copy(length_hbm, length_ref, query_sem.at[3]),
            pltpu.make_async_copy(owner_hbm, owner_ref, query_sem.at[4]),
            pltpu.make_async_copy(tag_hbm, tag_ref, query_sem.at[5]),
        )

    def start_loads(pair, _):
        for copy in loads(pair):
            copy.start()
        return 0

    lax.fori_loop(0, pairs, start_loads, 0)
    for copy in query_loads():
        copy.start()
    for slot, distance in enumerate(SLOTS):
        @pl.when(jnp.logical_not(inside(me + distance)))
        def _():
            window[:, slot] = jnp.zeros((pairs,) + window.shape[2:], window.dtype)

        @pl.when(jnp.logical_not(inside(me - distance)))
        def _():
            grad_in[:, slot] = jnp.zeros((pairs,) + grad_in.shape[2:], grad_in.dtype)

    barrier = pltpu.get_barrier_semaphore()
    for step in range(1, count):
        pl.semaphore_signal(
            barrier, inc=1, device_id={"seq": lax.rem(me + step, count)}, device_id_type=MESH
        )
    pl.semaphore_wait(barrier, count - 1)

    def send(pair, _):
        for copy in loads(pair):
            copy.wait()
        for step in range(levels):
            ctrl_copy(pair, step).start()
        for slot, distance in enumerate(SLOTS):
            @pl.when(inside(me - distance))
            def _():
                kv_copy(pair, slot).start()
        return 0

    lax.fori_loop(0, pairs, send, 0)

    for copy in query_loads():
        copy.wait()
    tubes = length_ref.shape[0]
    ends = []
    for tube in range(tubes):
        ends.append(length_ref[tube] + (ends[-1] if ends else 0))

    def tube_at(block):
        return sum(jnp.where(end <= block, 1, 0) for end in ends)

    mine = tube_at(me)
    owner = sum(jnp.where(mine == tube, owner_ref[tube], 0) for tube in range(tubes))
    lower2, lower, upper, upper2 = (
        inside(me + distance) & (tube_at(me + distance) == mine) for distance in SLOTS
    )
    first_bias = jnp.full((1, rows), jnp.where(lower | upper2, 0.0, MASKED), jnp.float32)
    second_bias = jnp.full((1, rows), jnp.where(upper | lower2, 0.0, MASKED), jnp.float32)
    own_bias = jnp.zeros((1, rows), jnp.float32)
    ctrl_open = tag_ref[...].reshape(1, count * ctrl_rows) == owner

    def bias_of(head):
        ctrl_bias = jnp.where(ctrl_open, bias_ref[head], MASKED)
        return jnp.concatenate([first_bias, own_bias, second_bias, ctrl_bias], axis=1)

    zero_block = jnp.zeros((rows, LANES), jnp.bfloat16)
    zero_grad = jnp.zeros((rows, LANES), jnp.float32)

    def relay(pair):
        for step in range(1, levels):
            ctrl_arrival(pair, step).wait_recv()
            ctrl_onward(pair, step).start()

    def column_sums(pair):
        mid_copy(pair).wait()
        ctrl_out[pair, column] = (
            ctrl_out[pair, column].astype(jnp.float32) + ctrl_mid[pair].astype(jnp.float32)
        ).astype(jnp.bfloat16)
        for step in range(1, levels):
            sum_copy(pair, step).start()

    def work(pair, _):
        @pl.when(pair + AHEAD < pairs)
        def _():
            relay(pair + AHEAD)

        ctrl_arrival(pair, 0).wait_recv()
        for step in range(1, levels):
            ctrl_onward_arrival(pair, step).wait_recv()
        for slot, distance in enumerate(SLOTS):
            @pl.when(inside(me + distance))
            def _():
                kv_copy(pair, slot).wait_recv()

        def gathered(kind):
            first = jnp.where(
                lower, window[pair, 1, kind], jnp.where(upper2, window[pair, 3, kind], zero_block)
            )
            second = jnp.where(
                upper, window[pair, 2, kind], jnp.where(lower2, window[pair, 0, kind], zero_block)
            )
            shared = ctrl[pair, :, kind].reshape(count * ctrl_rows, LANES)
            return jnp.concatenate([first, own[pair, kind], second, shared], axis=0)

        keys = gathered(0)
        values = gathered(1)
        q_two = masked_pair(q_ref[:, columns(pair)], low_lanes, 0.125)
        g_two = masked_pair(g_ref[:, columns(pair)], low_lanes, 1.0)
        scores = dot(q_two, keys, 1, 1)
        scores = jnp.concatenate(
            [scores[:rows] + bias_of(2 * pair), scores[rows:] + bias_of(2 * pair + 1)], axis=0
        )
        raised = jnp.exp(scores - jnp.max(scores, axis=1, keepdims=True))
        weights = raised * (1.0 / jnp.sum(raised, axis=1, keepdims=True))
        rounded = weights.astype(jnp.bfloat16)
        out_two = dot(rounded, values, 1, 0)
        attended = jnp.where(low_lanes, out_two[:rows], out_two[rows:]).astype(jnp.bfloat16)
        att_ref[:, columns(pair)] = attended
        attended = attended.astype(jnp.float32)
        delta = jnp.sum(
            g_two.astype(jnp.float32) * jnp.concatenate([attended, attended], axis=0),
            axis=1, keepdims=True,
        )
        d_scores = (weights * (dot(g_two, values, 1, 1) - delta)).astype(jnp.bfloat16)
        dq_two = dot(d_scores, keys, 1, 0) * 0.125
        dq_ref[:, columns(pair)] = jnp.where(low_lanes, dq_two[:rows], dq_two[rows:]).astype(
            jnp.bfloat16
        )
        for kind, grads in enumerate((dot(d_scores, q_two, 0, 0), dot(rounded, g_two, 0, 0))):
            first, second = grads[:rows], grads[2 * rows : 3 * rows]
            own_grad[pair, kind] = grads[rows : 2 * rows].astype(jnp.bfloat16)
            for slot, (chosen, term) in enumerate(
                ((lower2, second), (lower, first), (upper, second), (upper2, first))
            ):
                grad_out[pair, slot, kind] = jnp.where(chosen, term, zero_grad).astype(jnp.bfloat16)
            shared = grads[3 * rows :].astype(jnp.bfloat16)
            for device in range(count):
                ctrl_out[pair, device % 2, device // 2, kind] = (
                    shared[device * ctrl_rows : (device + 1) * ctrl_rows]
                )
        mid_copy(pair).start()
        for slot, distance in enumerate(SLOTS):
            @pl.when(inside(me + distance))
            def _():
                grad_copy(pair, slot).start()

        @pl.when(pair > 0)
        def _():
            column_sums(pair - 1)

        return 0

    for pair in range(AHEAD):
        relay(pair)
    lax.fori_loop(0, pairs, work, 0)
    column_sums(pairs - 1)

    def finish(pair, _):
        ctrl_in[pair, level] = ctrl_out[pair, column, level]
        for step in range(1, levels):
            sum_arrival(pair, step).wait_recv()
        for slot, distance in enumerate(SLOTS):
            @pl.when(inside(me - distance))
            def _():
                grad_copy(pair, slot).wait_recv()
        for kind, (key_ref, ctrl_ref) in enumerate(((dk_ref, dck_ref), (dv_ref, dcv_ref))):
            total = own_grad[pair, kind].astype(jnp.float32)
            for slot in range(len(SLOTS)):
                total += grad_in[pair, slot, kind].astype(jnp.float32)
            key_ref[:, columns(pair)] = total.astype(jnp.bfloat16)
            ctrl_total = ctrl_in[pair, 0, kind].astype(jnp.float32)
            for source in range(1, levels):
                ctrl_total += ctrl_in[pair, source, kind].astype(jnp.float32)
            ctrl_ref[:, columns(pair)] = ctrl_total.astype(jnp.bfloat16)
        return 0

    lax.fori_loop(0, pairs, finish, 0)

    def drain(pair, _):
        for step in range(levels):
            ctrl_copy(pair, step).wait_send()
        for step in range(1, levels):
            ctrl_onward(pair, step).wait_send()
            sum_copy(pair, step).wait_send()
        for slot, distance in enumerate(SLOTS):
            @pl.when(inside(me - distance))
            def _():
                kv_copy(pair, slot).wait_send()

            @pl.when(inside(me + distance))
            def _():
                grad_copy(pair, slot).wait_send()
        return 0

    lax.fori_loop(0, pairs, drain, 0)


def fused_shards(
    query_states, key_states, value_states, d_attended, ctrl_key, ctrl_value,
    ctrl_bias, tube_lengths, tube_owner, ctrl_owner,
):
    count = lax.axis_size("seq")
    rows, width = query_states.shape
    ctrl_rows = ctrl_key.shape[0]
    pairs = width // LANES
    vmem = pl.BlockSpec(memory_space=pltpu.VMEM)
    hbm = pl.BlockSpec(memory_space=pl.ANY)
    block = jax.ShapeDtypeStruct((rows, width), jnp.bfloat16)
    ctrl_block = jax.ShapeDtypeStruct((ctrl_rows, width), jnp.bfloat16)
    tile = (2, rows, LANES)
    ctrl_tile = (2, ctrl_rows, LANES)
    slots = len(SLOTS)
    results = pl.pallas_call(
        partial(tube_kernel, count),
        out_shape=(block, block, block, block, ctrl_block, ctrl_block),
        in_specs=[pl.BlockSpec(memory_space=pltpu.HBM)] * 10,
        out_specs=[vmem] * 6,
        scratch_shapes=[
            pltpu.VMEM((rows, width), jnp.bfloat16),
            pltpu.VMEM((rows, width), jnp.bfloat16),
            pltpu.VMEM((pairs,) + tile, jnp.bfloat16),
            pltpu.VMEM((pairs, slots) + tile, jnp.bfloat16),
            pltpu.VMEM((pairs, count) + ctrl_tile, jnp.bfloat16),
            pltpu.VMEM((pairs,) + tile, jnp.bfloat16),
            pltpu.VMEM((pairs, slots) + tile, jnp.bfloat16),
            pltpu.VMEM((pairs, slots) + tile, jnp.bfloat16),
            pltpu.VMEM((pairs, 2, count // 2) + ctrl_tile, jnp.bfloat16),
            pltpu.VMEM((pairs, count // 2) + ctrl_tile, jnp.bfloat16),
            pltpu.VMEM((pairs, count // 2) + ctrl_tile, jnp.bfloat16),
            pltpu.SMEM(ctrl_bias.shape, jnp.float32),
            pltpu.SMEM(tube_lengths.shape, jnp.int32),
            pltpu.SMEM(tube_owner.shape, jnp.int32),
            pltpu.VMEM(ctrl_owner.shape, jnp.int32),
            pltpu.SemaphoreType.DMA((pairs, 4)),
            pltpu.SemaphoreType.DMA((6,)),
            pltpu.SemaphoreType.DMA((pairs, slots)),
            pltpu.SemaphoreType.DMA((pairs, slots)),
            pltpu.SemaphoreType.DMA((pairs, count)),
            pltpu.SemaphoreType.DMA((pairs, count)),
            pltpu.SemaphoreType.DMA((pairs, slots)),
            pltpu.SemaphoreType.DMA((pairs, slots)),
            pltpu.SemaphoreType.DMA((pairs,)),
            pltpu.SemaphoreType.DMA((pairs,)),
            pltpu.SemaphoreType.DMA((pairs, count // 2)),
            pltpu.SemaphoreType.DMA((pairs, count // 2)),
        ],
        compiler_params=pltpu.CompilerParams(
            collective_id=0, has_side_effects=True, vmem_limit_bytes=64 * 1024 * 1024 - 65536
        ),
    )(
        query_states, key_states, value_states, d_attended, ctrl_key, ctrl_value,
        ctrl_bias, tube_lengths, tube_owner, ctrl_owner,
    )
    return pl.pallas_call(
        hand_over,
        out_shape=(block, block, block, block, ctrl_block, ctrl_block),
        in_specs=[hbm] * 6,
        out_specs=[hbm] * 6,
        scratch_shapes=[pltpu.VMEM(result.shape, result.dtype) for result in results]
        + [pltpu.SemaphoreType.DMA((6,)), pltpu.SemaphoreType.DMA((6,))],
        compiler_params=pltpu.CompilerParams(vmem_limit_bytes=64 * 1024 * 1024 - 65536),
    )(*results)


def hand_over(*refs):
    loaded, load_sems, store_sems = refs[12:18], refs[18], refs[19]
    copies_in = [
        pltpu.make_async_copy(refs[i], loaded[i], load_sems.at[i]) for i in range(6)
    ]
    copies_out = [
        pltpu.make_async_copy(loaded[i], refs[6 + i], store_sems.at[i]) for i in range(6)
    ]
    for copy in copies_in:
        copy.start()
    for copy_in, copy_out in zip(copies_in, copies_out):
        copy_in.wait()
        copy_out.start()
    for copy in copies_out:
        copy.wait()


def fused_or_plain(*arrays):
    tile_rows = 16
    fits = arrays[4].shape[0] % tile_rows == 0 and arrays[0].shape[0] == BLK
    return (fused_shards if fits else shards)(*arrays)


def solution(mesh):
    return jax.shard_map(
        fused_or_plain,
        mesh=mesh,
        in_specs=(
            P(("groups", "seq"), "head"),
            P(("groups", "seq"), "head"),
            P(("groups", "seq"), "head"),
            P(("groups", "seq"), "head"),
            P(("groups", "seq"), "head"),
            P(("groups", "seq"), "head"),
            P("head"),
            P("groups"),
            P("groups"),
            P("groups"),
        ),
        out_specs=(
            P(("groups", "seq"), "head"),
            P(("groups", "seq"), "head"),
            P(("groups", "seq"), "head"),
            P(("groups", "seq"), "head"),
            P(("groups", "seq"), "head"),
            P(("groups", "seq"), "head"),
        ),
        check_vma=False,
    )
```

```python
from functools import partial

import jax
import jax.numpy as jnp
from jax import lax
from jax.experimental import pallas as pl
from jax.experimental.pallas import tpu as pltpu
from jax.sharding import PartitionSpec as P

BLK = 128
REACH = 2


MASKED = -1e30


def passed_along(block, axis, distance):
    devices = range(lax.axis_size(axis))
    route = [(i - distance, i) for i in devices if i - distance in devices]
    return lax.ppermute(block, axis, route)


def tube_tables(tube_lengths, tube_owner, blocks_all):
    tube_ends = jnp.cumsum(tube_lengths, dtype=jnp.int32)
    blocks = jnp.arange(blocks_all, dtype=jnp.int32)
    tube_index = jnp.sum(
        (tube_ends[None, :] <= blocks[:, None]).astype(jnp.int32), axis=1, dtype=jnp.int32
    )
    tube_ids = jnp.arange(tube_lengths.shape[0], dtype=jnp.int32)
    matches = tube_ids[None, :] == tube_index[:, None]
    owner_index = jnp.sum(jnp.where(matches, tube_owner[None, :], 0), axis=1, dtype=jnp.int32)
    return (tube_index, owner_index)


def split_heads(rows_in, head_width):
    return rows_in.reshape(rows_in.shape[0], rows_in.shape[1] // head_width, head_width)


def scores_of(q_blk, k_blk):
    return jnp.einsum(
        "qhd,khd->hqk", q_blk, k_blk, preferred_element_type=jnp.float32
    ) * q_blk.shape[-1] ** (-0.5)


def weights_of(scores, row_high, row_total):
    return jnp.exp(scores - row_high[..., None]) / row_total[..., None]


def raise_stats(statistics, scores):
    row_high, row_total = statistics
    new_high = jnp.maximum(row_high, jnp.max(scores, axis=-1))
    row_total = row_total * jnp.exp(row_high - new_high) + jnp.sum(
        jnp.exp(scores - new_high[..., None]), axis=-1
    )
    return (new_high, row_total)


def unchanged(carried):
    return carried


def round_trip(values):
    return lax.optimization_barrier(values.astype(jnp.bfloat16)).astype(jnp.float32)


def shards(
    query_states,
    key_states,
    value_states,
    d_attended,
    ctrl_key,
    ctrl_value,
    ctrl_bias,
    tube_lengths,
    tube_owner,
    ctrl_owner,
):
    row_count, width_all = query_states.shape
    head_width = width_all // ctrl_bias.shape[0]
    head_scale = head_width ** (-0.5)
    per_device = row_count // BLK
    blocks_all = lax.axis_size("seq") * per_device
    position = lax.axis_index("seq")
    slot_count = 2 * REACH + 1
    tube_index, owner_index = tube_tables(tube_lengths, tube_owner, blocks_all)
    ctrl_pair = lax.all_gather(jnp.stack([ctrl_key, ctrl_value]), "seq", axis=1, tiled=True)
    ctrl_keys = split_heads(ctrl_pair[0], head_width)
    ctrl_values = split_heads(ctrl_pair[1], head_width)
    ctrl_shift = ctrl_bias[:, None, None]
    key_value = jnp.stack([key_states, value_states])
    lower_side = [passed_along(key_value, "seq", distance) for distance in range(REACH, 0, -1)]
    upper_side = [passed_along(key_value, "seq", -distance) for distance in range(1, REACH + 1)]
    kv_window = lower_side + [key_value] + upper_side

    def member(slot_index, block_local, tube_id):
        block_id = (position - REACH + slot_index) * per_device + block_local
        clipped = jnp.clip(block_id, 0, blocks_all - 1)
        return (block_id >= 0) & (block_id < blocks_all) & (tube_index[clipped] == tube_id)

    def window_block(window, slot_index, block_local, member_index):
        return split_heads(
            window[slot_index][member_index, block_local * BLK : (block_local + 1) * BLK],
            head_width,
        )

    def visit_keys(update, carried, tube_id, skipped):
        for slot_index in range(slot_count):
            for key_local in range(per_device):
                if slot_index == REACH and key_local == skipped:
                    continue
                carried = lax.cond(
                    member(slot_index, key_local, tube_id),
                    partial(update, slot_index=slot_index, key_local=key_local),
                    unchanged,
                    carried,
                )
        return carried

    q_blocks, g_blocks, query_tubes, ctrl_masks = ([], [], [], [])
    query_local = 0
    q_blocks.append(split_heads(query_states, head_width))
    g_blocks.append(split_heads(d_attended, head_width))
    block_id = position * per_device + query_local
    query_tubes.append(tube_index[block_id])
    ctrl_masks.append((ctrl_owner == owner_index[block_id])[None, None, :])

    def ctrl_scores(query_local):
        return jnp.where(
            ctrl_masks[query_local],
            scores_of(q_blocks[query_local], ctrl_keys) + ctrl_shift,
            MASKED,
        )

    highs, totals, deltas, attended_blocks = ([], [], [], [])
    query_local = 0
    q_blk = q_blocks[query_local]
    own_scores = scores_of(q_blk, window_block(kv_window, REACH, query_local, 0))
    row_high = jnp.max(own_scores, axis=-1)
    statistics = (row_high, jnp.sum(jnp.exp(own_scores - row_high[..., None]), axis=-1))
    statistics = raise_stats(statistics, ctrl_scores(query_local))

    def add_stats(carried, slot_index, key_local, q_blk=q_blk):
        return raise_stats(
            carried, scores_of(q_blk, window_block(kv_window, slot_index, key_local, 0))
        )

    row_high, row_total = visit_keys(add_stats, statistics, query_tubes[query_local], query_local)
    ctrl_weights = weights_of(ctrl_scores(query_local), row_high, row_total).astype(jnp.bfloat16)
    summed = jnp.einsum(
        "hqk,khd->qhd", ctrl_weights, ctrl_values, preferred_element_type=jnp.float32
    )

    def add_values(
        carried, slot_index, key_local, q_blk=q_blk, row_high=row_high, row_total=row_total
    ):
        k_blk = window_block(kv_window, slot_index, key_local, 0)
        v_blk = window_block(kv_window, slot_index, key_local, 1)
        weights = weights_of(scores_of(q_blk, k_blk), row_high, row_total).astype(jnp.bfloat16)
        return carried + jnp.einsum(
            "hqk,khd->qhd", weights, v_blk, preferred_element_type=jnp.float32
        )

    summed = visit_keys(add_values, summed, query_tubes[query_local], -1)
    attended_blk = summed.astype(jnp.bfloat16)
    row_delta = jnp.sum(
        g_blocks[query_local].astype(jnp.float32) * attended_blk.astype(jnp.float32), axis=-1
    ).T
    highs.append(row_high)
    totals.append(row_total)
    deltas.append(row_delta)
    attended_blocks.append(attended_blk)

    def grad_terms(query_local, v_blk, scores):
        weights = weights_of(scores, highs[query_local], totals[query_local])
        d_prob = jnp.einsum(
            "qhd,khd->hqk", g_blocks[query_local], v_blk, preferred_element_type=jnp.float32
        )
        d_scores = (weights * (d_prob - deltas[query_local][..., None])).astype(jnp.bfloat16)
        return (weights.astype(jnp.bfloat16), d_scores)

    query_local = 0
    rounded, d_scores = grad_terms(query_local, ctrl_values, ctrl_scores(query_local))
    d_queries = [
        jnp.einsum("hqk,khd->qhd", d_scores, ctrl_keys, preferred_element_type=jnp.float32)
        * head_scale
    ]
    ctrl_key_grad = (
        jnp.einsum(
            "hqk,qhd->khd", d_scores, q_blocks[query_local], preferred_element_type=jnp.float32
        )
        * head_scale
    )
    ctrl_value_grad = jnp.einsum(
        "hqk,qhd->khd", rounded, g_blocks[query_local], preferred_element_type=jnp.float32
    )
    block_zeros = jnp.zeros((BLK, width_all // head_width, head_width), jnp.float32)
    key_parts = jnp.zeros((2, row_count, width_all), jnp.float32)
    for slot_index in range(slot_count):
        key_local = 0
        k_blk = window_block(kv_window, slot_index, key_local, 0)
        v_blk = window_block(kv_window, slot_index, key_local, 1)
        key_grad = block_zeros
        value_grad = block_zeros
        query_local = 0

        def add_grads(carried, query_local=query_local, k_blk=k_blk, v_blk=v_blk):
            rounded, d_scores = grad_terms(
                query_local, v_blk, scores_of(q_blocks[query_local], k_blk)
            )
            d_query_blk = (
                carried[0]
                + jnp.einsum("hqk,khd->qhd", d_scores, k_blk, preferred_element_type=jnp.float32)
                * head_scale
            )
            key_term = (
                jnp.einsum(
                    "hqk,qhd->khd",
                    d_scores,
                    q_blocks[query_local],
                    preferred_element_type=jnp.float32,
                )
                * head_scale
            )
            value_term = jnp.einsum(
                "hqk,qhd->khd", rounded, g_blocks[query_local], preferred_element_type=jnp.float32
            )
            return (d_query_blk, key_term, value_term)

        carried = lax.cond(
            member(slot_index, key_local, query_tubes[query_local]),
            add_grads,
            unchanged,
            (d_queries[query_local], key_grad, value_grad),
        )
        d_queries[query_local], key_grad, value_grad = carried
        slot_pieces = jnp.stack([key_grad, value_grad]).reshape(2, BLK, width_all)
        if slot_index == REACH:
            key_parts = key_parts + round_trip(slot_pieces)
        else:
            received = passed_along(slot_pieces.astype(jnp.bfloat16), "seq", slot_index - REACH)
            key_parts = key_parts + received.astype(jnp.float32)
    key_results = key_parts.astype(jnp.bfloat16)
    ctrl_terms = jnp.stack(
        [ctrl_key_grad.reshape(-1, width_all), ctrl_value_grad.reshape(-1, width_all)]
    )
    ctrl_results = lax.psum_scatter(ctrl_terms, "seq", scatter_dimension=1, tiled=True).astype(
        jnp.bfloat16
    )
    attended = attended_blocks[0].reshape(row_count, width_all)
    d_query = d_queries[0].reshape(row_count, width_all).astype(jnp.bfloat16)
    return (attended, d_query, key_results[0], key_results[1], ctrl_results[0], ctrl_results[1])


MESH = pl.DeviceIdType.MESH
SLOTS = (-2, -1, 1, 2)
LANES = 128
AHEAD = 2


def masked_pair(rows, low_lanes, factor):
    first = low_lanes.astype(jnp.float32) * factor
    second = factor - first
    return jnp.concatenate(
        [rows * first.astype(rows.dtype), rows * second.astype(rows.dtype)], axis=0
    )


def dot(left, right, left_dim, right_dim):
    return lax.dot_general(
        left, right, (((left_dim,), (right_dim,)), ((), ())), preferred_element_type=jnp.float32
    )


def tube_kernel(
    count, q_hbm, k_hbm, v_hbm, g_hbm, ck_hbm, cv_hbm,
    bias_hbm, length_hbm, owner_hbm, tag_hbm,
    att_ref, dq_ref, dk_ref, dv_ref, dck_ref, dcv_ref,
    q_ref, g_ref, own, window, ctrl, own_grad, grad_out, grad_mid, grad_in, ctrl_out, ctrl_mid, ctrl_in,
    bias_ref, length_ref, owner_ref, tag_ref, load_sem, query_sem,
    kv_send, kv_recv, ctrl_send, ctrl_recv, grad_send, grad_recv,
    mid_send, mid_recv, sum_send, sum_recv, part_send, part_recv,
):
    me = lax.axis_index("seq")
    column = lax.rem(me, 2)
    side = 1 - 2 * column
    peer = me + side
    near, across, far, back = 2 - column, 1 + column, 3 - 3 * column, 3 * column
    level = me // 2
    levels = count // 2
    rows = q_ref.shape[0]
    ctrl_rows = ck_hbm.shape[0]
    pairs = q_ref.shape[1] // LANES
    low_lanes = lax.broadcasted_iota(jnp.int32, (1, LANES), 1) < LANES // 2

    def inside(device):
        return (device >= 0) & (device < count)

    def columns(pair):
        return pl.ds(pl.multiple_of(pair * LANES, LANES), LANES)

    def kv_copy(pair, slot, distance):
        return pltpu.make_async_remote_copy(
            own.at[pair], window.at[pair, slot], kv_send.at[pair, slot], kv_recv.at[pair, slot],
            device_id={"seq": me - distance}, device_id_type=MESH,
        )

    def kv_arrival(pair, slot):
        return kv_copy(pair, slot, -side)

    def kv_onward(pair, by_peer):
        source, target = (far, near) if by_peer else (near, across)
        return pltpu.make_async_remote_copy(
            window.at[pair, source], window.at[pair, target],
            kv_send.at[pair, near], kv_recv.at[pair, target],
            device_id={"seq": peer if by_peer else me + 2 * side}, device_id_type=MESH,
        )

    def grad_copy(pair, slot, distance):
        return pltpu.make_async_remote_copy(
            grad_out.at[pair, slot], grad_in.at[pair, slot],
            grad_send.at[pair, slot], grad_recv.at[pair, slot],
            device_id={"seq": me + distance}, device_id_type=MESH,
        )

    def grad_arrival(pair, slot):
        return grad_copy(pair, slot, side)

    def part_copy(pair, by_peer):
        return pltpu.make_async_remote_copy(
            grad_out.at[pair, across], grad_mid.at[pair], part_send.at[pair], part_recv.at[pair],
            device_id={"seq": peer if by_peer else me - 2 * side}, device_id_type=MESH,
        )

    has_far, has_back = inside(me + 2 * side), inside(me - 2 * side)

    def by_parity(pair, act):
        even = lax.rem(pair, 2) == 0

        @pl.when(even)
        def _():
            act(True)

        @pl.when(jnp.logical_not(even))
        def _():
            act(False)

    def mate(step):
        return lax.rem(me + 2 * step, count)

    def mate_before(step):
        return lax.rem(me - 2 * step + count, count)

    def ctrl_copy(pair, step):
        return pltpu.make_async_remote_copy(
            ctrl.at[pair, me], ctrl.at[pair, me], ctrl_send.at[pair, step], ctrl_recv.at[pair, step],
            device_id={"seq": mate(step) if step else peer}, device_id_type=MESH,
        )

    def ctrl_arrival(pair, step):
        source = mate_before(step) if step else peer
        return pltpu.make_async_remote_copy(
            ctrl.at[pair, source], ctrl.at[pair, source],
            ctrl_send.at[pair, step], ctrl_recv.at[pair, step],
            device_id={"seq": source}, device_id_type=MESH,
        )

    def ctrl_onward(pair, step):
        source = mate_before(step)
        return pltpu.make_async_remote_copy(
            ctrl.at[pair, source], ctrl.at[pair, source],
            ctrl_send.at[pair, levels + step], ctrl_recv.at[pair, levels + step],
            device_id={"seq": peer}, device_id_type=MESH,
        )

    def ctrl_onward_arrival(pair, step):
        source = mate_before(step) + 1 - 2 * column
        return pltpu.make_async_remote_copy(
            ctrl.at[pair, source], ctrl.at[pair, source],
            ctrl_send.at[pair, levels + step], ctrl_recv.at[pair, levels + step],
            device_id={"seq": peer}, device_id_type=MESH,
        )

    def mid_copy(pair):
        return pltpu.make_async_remote_copy(
            ctrl_out.at[pair, 1 - column], ctrl_mid.at[pair], mid_send.at[pair], mid_recv.at[pair],
            device_id={"seq": peer}, device_id_type=MESH,
        )

    def sum_copy(pair, step):
        return pltpu.make_async_remote_copy(
            ctrl_out.at[pair, column, mate(step) // 2], ctrl_in.at[pair, level],
            sum_send.at[pair, step], sum_recv.at[pair, step],
            device_id={"seq": mate(step)}, device_id_type=MESH,
        )

    def sum_arrival(pair, step):
        source = mate_before(step)
        return pltpu.make_async_remote_copy(
            ctrl_out.at[pair, column, level], ctrl_in.at[pair, source // 2],
            sum_send.at[pair, step], sum_recv.at[pair, step],
            device_id={"seq": source}, device_id_type=MESH,
        )

    def loads(pair):
        part = columns(pair)
        return [
            pltpu.make_async_copy(source.at[:, part], target, load_sem.at[pair, i])
            for i, (source, target) in enumerate((
                (ck_hbm, ctrl.at[pair, me, 0]), (cv_hbm, ctrl.at[pair, me, 1]),
                (k_hbm, own.at[pair, 0]), (v_hbm, own.at[pair, 1]),
            ))
        ]

    def query_loads():
        return (
            pltpu.make_async_copy(q_hbm, q_ref, query_sem.at[0]),
            pltpu.make_async_copy(g_hbm, g_ref, query_sem.at[1]),
            pltpu.make_async_copy(bias_hbm, bias_ref, query_sem.at[2]),
            pltpu.make_async_copy(length_hbm, length_ref, query_sem.at[3]),
            pltpu.make_async_copy(owner_hbm, owner_ref, query_sem.at[4]),
            pltpu.make_async_copy(tag_hbm, tag_ref, query_sem.at[5]),
        )

    def start_loads(pair, _):
        for copy in loads(pair):
            copy.start()
        return 0

    lax.fori_loop(0, pairs, start_loads, 0)
    for copy in query_loads():
        copy.start()
    for slot, distance in enumerate(SLOTS):
        @pl.when(jnp.logical_not(inside(me + distance)))
        def _():
            window[:, slot] = jnp.zeros((pairs,) + window.shape[2:], window.dtype)

        @pl.when(jnp.logical_not(inside(me - distance)) | (near == slot))
        def _():
            grad_in[:, slot] = jnp.zeros((pairs,) + grad_in.shape[2:], grad_in.dtype)

    barrier = pltpu.get_barrier_semaphore()
    for step in range(1, count):
        pl.semaphore_signal(
            barrier, inc=1, device_id={"seq": lax.rem(me + step, count)}, device_id_type=MESH
        )
    pl.semaphore_wait(barrier, count - 1)

    def send(pair, _):
        for copy in loads(pair):
            copy.wait()
        kv_copy(pair, across, -side).start()

        @pl.when(has_far)
        def _():
            kv_copy(pair, back, -2 * side).start()

        @pl.when(has_back)
        def _():
            kv_copy(pair, far, 2 * side).start()

        for step in range(levels):
            ctrl_copy(pair, step).start()
        return 0

    lax.fori_loop(0, pairs, send, 0)

    for copy in query_loads():
        copy.wait()
    tubes = length_ref.shape[0]
    ends = []
    for tube in range(tubes):
        ends.append(length_ref[tube] + (ends[-1] if ends else 0))

    def tube_at(block):
        return sum(jnp.where(end <= block, 1, 0) for end in ends)

    mine = tube_at(me)
    owner = sum(jnp.where(mine == tube, owner_ref[tube], 0) for tube in range(tubes))
    lower2, lower, upper, upper2 = (
        inside(me + distance) & (tube_at(me + distance) == mine) for distance in SLOTS
    )
    first_bias = jnp.full((1, rows), jnp.where(lower | upper2, 0.0, MASKED), jnp.float32)
    second_bias = jnp.full((1, rows), jnp.where(upper | lower2, 0.0, MASKED), jnp.float32)
    own_bias = jnp.zeros((1, rows), jnp.float32)
    ctrl_open = tag_ref[...].reshape(1, count * ctrl_rows) == owner

    def bias_of(head):
        ctrl_bias = jnp.where(ctrl_open, bias_ref[head], MASKED)
        return jnp.concatenate([first_bias, own_bias, second_bias, ctrl_bias], axis=1)

    zero_block = jnp.zeros((rows, LANES), jnp.bfloat16)
    zero_grad = jnp.zeros((rows, LANES), jnp.float32)

    def relay(pair):
        for step in range(1, levels):
            ctrl_arrival(pair, step).wait_recv()
            ctrl_onward(pair, step).start()

        def act(by_peer):
            if not by_peer:
                kv_arrival(pair, near).wait_recv()

            @pl.when(has_far)
            def _():
                if by_peer:
                    kv_arrival(pair, far).wait_recv()
                kv_onward(pair, by_peer).start()

        by_parity(pair, act)

    def column_sums(pair):
        mid_copy(pair).wait()
        ctrl_out[pair, column] = (
            ctrl_out[pair, column].astype(jnp.float32) + ctrl_mid[pair].astype(jnp.float32)
        ).astype(jnp.bfloat16)
        for step in range(1, levels):
            sum_copy(pair, step).start()

        def act(by_peer):
            slot = far if by_peer else near

            @pl.when(has_far)
            def _():
                part_copy(pair, True).wait_recv()
                grad_out[pair, slot] = (
                    grad_out[pair, slot].astype(jnp.float32) + grad_mid[pair].astype(jnp.float32)
                ).astype(jnp.bfloat16)

            if by_peer:
                @pl.when(has_far)
                def _():
                    grad_copy(pair, far, 2 * side).start()
            else:
                grad_copy(pair, near, side).start()

        by_parity(pair, act)

    def work(pair, _):
        @pl.when(pair + AHEAD < pairs)
        def _():
            relay(pair + AHEAD)

        ctrl_arrival(pair, 0).wait_recv()
        for step in range(1, levels):
            ctrl_onward_arrival(pair, step).wait_recv()
        def await_rest(by_peer):
            if by_peer:
                kv_arrival(pair, near).wait_recv()
            else:
                @pl.when(has_far)
                def _():
                    kv_arrival(pair, far).wait_recv()

        by_parity(pair, await_rest)

        @pl.when(has_back)
        def _():
            kv_arrival(pair, back).wait_recv()
            kv_arrival(pair, across).wait_recv()

        def gathered(kind):
            first = jnp.where(
                lower, window[pair, 1, kind], jnp.where(upper2, window[pair, 3, kind], zero_block)
            )
            second = jnp.where(
                upper, window[pair, 2, kind], jnp.where(lower2, window[pair, 0, kind], zero_block)
            )
            shared = ctrl[pair, :, kind].reshape(count * ctrl_rows, LANES)
            return jnp.concatenate([first, own[pair, kind], second, shared], axis=0)

        keys = gathered(0)
        values = gathered(1)
        q_two = masked_pair(q_ref[:, columns(pair)], low_lanes, 0.125)
        g_two = masked_pair(g_ref[:, columns(pair)], low_lanes, 1.0)
        scores = dot(q_two, keys, 1, 1)
        scores = jnp.concatenate(
            [scores[:rows] + bias_of(2 * pair), scores[rows:] + bias_of(2 * pair + 1)], axis=0
        )
        raised = jnp.exp(scores - jnp.max(scores, axis=1, keepdims=True))
        weights = raised * (1.0 / jnp.sum(raised, axis=1, keepdims=True))
        rounded = weights.astype(jnp.bfloat16)
        out_two = dot(rounded, values, 1, 0)
        attended = jnp.where(low_lanes, out_two[:rows], out_two[rows:]).astype(jnp.bfloat16)
        att_ref[:, columns(pair)] = attended
        attended = attended.astype(jnp.float32)
        delta = jnp.sum(
            g_two.astype(jnp.float32) * jnp.concatenate([attended, attended], axis=0),
            axis=1, keepdims=True,
        )
        d_scores = (weights * (dot(g_two, values, 1, 1) - delta)).astype(jnp.bfloat16)
        dq_two = dot(d_scores, keys, 1, 0) * 0.125
        dq_ref[:, columns(pair)] = jnp.where(low_lanes, dq_two[:rows], dq_two[rows:]).astype(
            jnp.bfloat16
        )
        for kind, grads in enumerate((dot(d_scores, q_two, 0, 0), dot(rounded, g_two, 0, 0))):
            first, second = grads[:rows], grads[2 * rows : 3 * rows]
            own_grad[pair, kind] = grads[rows : 2 * rows].astype(jnp.bfloat16)
            for slot, (chosen, term) in enumerate(
                ((lower2, second), (lower, first), (upper, second), (upper2, first))
            ):
                grad_out[pair, slot, kind] = jnp.where(chosen, term, zero_grad).astype(jnp.bfloat16)
            shared = grads[3 * rows :].astype(jnp.bfloat16)
            for device in range(count):
                ctrl_out[pair, device % 2, device // 2, kind] = (
                    shared[device * ctrl_rows : (device + 1) * ctrl_rows]
                )
        mid_copy(pair).start()

        def hand_on(by_peer):
            @pl.when(has_back)
            def _():
                part_copy(pair, by_peer).start()
                grad_copy(pair, back, -2 * side).start()

            if by_peer:
                grad_copy(pair, near, side).start()
            else:
                @pl.when(has_far)
                def _():
                    grad_copy(pair, far, 2 * side).start()

        by_parity(pair, hand_on)

        @pl.when(pair > 0)
        def _():
            column_sums(pair - 1)

        return 0

    for pair in range(AHEAD):
        relay(pair)
    lax.fori_loop(0, pairs, work, 0)
    column_sums(pairs - 1)

    def finish(pair, _):
        ctrl_in[pair, level] = ctrl_out[pair, column, level]
        for step in range(1, levels):
            sum_arrival(pair, step).wait_recv()
        grad_arrival(pair, across).wait_recv()

        @pl.when(has_back)
        def _():
            grad_arrival(pair, far).wait_recv()

        @pl.when(has_far)
        def _():
            grad_arrival(pair, back).wait_recv()

        for kind, (key_ref, ctrl_ref) in enumerate(((dk_ref, dck_ref), (dv_ref, dcv_ref))):
            total = own_grad[pair, kind].astype(jnp.float32)
            for slot in range(len(SLOTS)):
                total += grad_in[pair, slot, kind].astype(jnp.float32)
            key_ref[:, columns(pair)] = total.astype(jnp.bfloat16)
            ctrl_total = ctrl_in[pair, 0, kind].astype(jnp.float32)
            for source in range(1, levels):
                ctrl_total += ctrl_in[pair, source, kind].astype(jnp.float32)
            ctrl_ref[:, columns(pair)] = ctrl_total.astype(jnp.bfloat16)
        return 0

    lax.fori_loop(0, pairs, finish, 0)

    def drain(pair, _):
        for step in range(levels):
            ctrl_copy(pair, step).wait_send()
        for step in range(1, levels):
            ctrl_onward(pair, step).wait_send()
            sum_copy(pair, step).wait_send()
        kv_copy(pair, across, -side).wait_send()
        grad_copy(pair, near, side).wait_send()

        @pl.when(has_far)
        def _():
            kv_copy(pair, back, -2 * side).wait_send()
            kv_onward(pair, True).wait_send()
            grad_copy(pair, far, 2 * side).wait_send()

        @pl.when(has_back)
        def _():
            kv_copy(pair, far, 2 * side).wait_send()
            part_copy(pair, True).wait_send()
            grad_copy(pair, back, -2 * side).wait_send()

        return 0

    lax.fori_loop(0, pairs, drain, 0)


def fused_shards(
    query_states, key_states, value_states, d_attended, ctrl_key, ctrl_value,
    ctrl_bias, tube_lengths, tube_owner, ctrl_owner,
):
    count = lax.axis_size("seq")
    rows, width = query_states.shape
    ctrl_rows = ctrl_key.shape[0]
    pairs = width // LANES
    vmem = pl.BlockSpec(memory_space=pltpu.VMEM)
    hbm = pl.BlockSpec(memory_space=pl.ANY)
    block = jax.ShapeDtypeStruct((rows, width), jnp.bfloat16)
    ctrl_block = jax.ShapeDtypeStruct((ctrl_rows, width), jnp.bfloat16)
    tile = (2, rows, LANES)
    ctrl_tile = (2, ctrl_rows, LANES)
    slots = len(SLOTS)
    results = pl.pallas_call(
        partial(tube_kernel, count),
        out_shape=(block, block, block, block, ctrl_block, ctrl_block),
        in_specs=[pl.BlockSpec(memory_space=pltpu.HBM)] * 10,
        out_specs=[vmem] * 6,
        scratch_shapes=[
            pltpu.VMEM((rows, width), jnp.bfloat16),
            pltpu.VMEM((rows, width), jnp.bfloat16),
            pltpu.VMEM((pairs,) + tile, jnp.bfloat16),
            pltpu.VMEM((pairs, slots) + tile, jnp.bfloat16),
            pltpu.VMEM((pairs, count) + ctrl_tile, jnp.bfloat16),
            pltpu.VMEM((pairs,) + tile, jnp.bfloat16),
            pltpu.VMEM((pairs, slots) + tile, jnp.bfloat16),
            pltpu.VMEM((pairs,) + tile, jnp.bfloat16),
            pltpu.VMEM((pairs, slots) + tile, jnp.bfloat16),
            pltpu.VMEM((pairs, 2, count // 2) + ctrl_tile, jnp.bfloat16),
            pltpu.VMEM((pairs, count // 2) + ctrl_tile, jnp.bfloat16),
            pltpu.VMEM((pairs, count // 2) + ctrl_tile, jnp.bfloat16),
            pltpu.SMEM(ctrl_bias.shape, jnp.float32),
            pltpu.SMEM(tube_lengths.shape, jnp.int32),
            pltpu.SMEM(tube_owner.shape, jnp.int32),
            pltpu.VMEM(ctrl_owner.shape, jnp.int32),
            pltpu.SemaphoreType.DMA((pairs, 4)),
            pltpu.SemaphoreType.DMA((6,)),
            pltpu.SemaphoreType.DMA((pairs, slots)),
            pltpu.SemaphoreType.DMA((pairs, slots)),
            pltpu.SemaphoreType.DMA((pairs, count)),
            pltpu.SemaphoreType.DMA((pairs, count)),
            pltpu.SemaphoreType.DMA((pairs, slots)),
            pltpu.SemaphoreType.DMA((pairs, slots)),
            pltpu.SemaphoreType.DMA((pairs,)),
            pltpu.SemaphoreType.DMA((pairs,)),
            pltpu.SemaphoreType.DMA((pairs, count // 2)),
            pltpu.SemaphoreType.DMA((pairs, count // 2)),
            pltpu.SemaphoreType.DMA((pairs,)),
            pltpu.SemaphoreType.DMA((pairs,)),
        ],
        compiler_params=pltpu.CompilerParams(
            collective_id=0, has_side_effects=True, vmem_limit_bytes=64 * 1024 * 1024 - 65536
        ),
    )(
        query_states, key_states, value_states, d_attended, ctrl_key, ctrl_value,
        ctrl_bias, tube_lengths, tube_owner, ctrl_owner,
    )
    return pl.pallas_call(
        hand_over,
        out_shape=(block, block, block, block, ctrl_block, ctrl_block),
        in_specs=[hbm] * 6,
        out_specs=[hbm] * 6,
        scratch_shapes=[pltpu.VMEM(result.shape, result.dtype) for result in results]
        + [pltpu.SemaphoreType.DMA((6,)), pltpu.SemaphoreType.DMA((6,))],
        compiler_params=pltpu.CompilerParams(vmem_limit_bytes=64 * 1024 * 1024 - 65536),
    )(*results)


def hand_over(*refs):
    loaded, load_sems, store_sems = refs[12:18], refs[18], refs[19]
    copies_in = [
        pltpu.make_async_copy(refs[i], loaded[i], load_sems.at[i]) for i in range(6)
    ]
    copies_out = [
        pltpu.make_async_copy(loaded[i], refs[6 + i], store_sems.at[i]) for i in range(6)
    ]
    for copy in copies_in:
        copy.start()
    for copy_in, copy_out in zip(copies_in, copies_out):
        copy_in.wait()
        copy_out.start()
    for copy in copies_out:
        copy.wait()


def fused_or_plain(*arrays):
    tile_rows = 16
    fits = arrays[4].shape[0] % tile_rows == 0 and arrays[0].shape[0] == BLK
    return (fused_shards if fits else shards)(*arrays)


def solution(mesh):
    return jax.shard_map(
        fused_or_plain,
        mesh=mesh,
        in_specs=(
            P(("groups", "seq"), "head"),
            P(("groups", "seq"), "head"),
            P(("groups", "seq"), "head"),
            P(("groups", "seq"), "head"),
            P(("groups", "seq"), "head"),
            P(("groups", "seq"), "head"),
            P("head"),
            P("groups"),
            P("groups"),
            P("groups"),
        ),
        out_specs=(
            P(("groups", "seq"), "head"),
            P(("groups", "seq"), "head"),
            P(("groups", "seq"), "head"),
            P(("groups", "seq"), "head"),
            P(("groups", "seq"), "head"),
            P(("groups", "seq"), "head"),
        ),
        check_vma=False,
    )
```

```python
from functools import partial

import jax
import jax.numpy as jnp
from jax import lax
from jax.experimental import pallas as pl
from jax.experimental.pallas import tpu as pltpu
from jax.sharding import PartitionSpec as P

BLK = 128
REACH = 2


MASKED = -1e30


def passed_along(block, axis, distance):
    devices = range(lax.axis_size(axis))
    route = [(i - distance, i) for i in devices if i - distance in devices]
    return lax.ppermute(block, axis, route)


def tube_tables(tube_lengths, tube_owner, blocks_all):
    tube_ends = jnp.cumsum(tube_lengths, dtype=jnp.int32)
    blocks = jnp.arange(blocks_all, dtype=jnp.int32)
    tube_index = jnp.sum(
        (tube_ends[None, :] <= blocks[:, None]).astype(jnp.int32), axis=1, dtype=jnp.int32
    )
    tube_ids = jnp.arange(tube_lengths.shape[0], dtype=jnp.int32)
    matches = tube_ids[None, :] == tube_index[:, None]
    owner_index = jnp.sum(jnp.where(matches, tube_owner[None, :], 0), axis=1, dtype=jnp.int32)
    return (tube_index, owner_index)


def split_heads(rows_in, head_width):
    return rows_in.reshape(rows_in.shape[0], rows_in.shape[1] // head_width, head_width)


def scores_of(q_blk, k_blk):
    return jnp.einsum(
        "qhd,khd->hqk", q_blk, k_blk, preferred_element_type=jnp.float32
    ) * q_blk.shape[-1] ** (-0.5)


def weights_of(scores, row_high, row_total):
    return jnp.exp(scores - row_high[..., None]) / row_total[..., None]


def raise_stats(statistics, scores):
    row_high, row_total = statistics
    new_high = jnp.maximum(row_high, jnp.max(scores, axis=-1))
    row_total = row_total * jnp.exp(row_high - new_high) + jnp.sum(
        jnp.exp(scores - new_high[..., None]), axis=-1
    )
    return (new_high, row_total)


def unchanged(carried):
    return carried


def round_trip(values):
    return lax.optimization_barrier(values.astype(jnp.bfloat16)).astype(jnp.float32)


def shards(
    query_states,
    key_states,
    value_states,
    d_attended,
    ctrl_key,
    ctrl_value,
    ctrl_bias,
    tube_lengths,
    tube_owner,
    ctrl_owner,
):
    row_count, width_all = query_states.shape
    head_width = width_all // ctrl_bias.shape[0]
    head_scale = head_width ** (-0.5)
    per_device = row_count // BLK
    blocks_all = lax.axis_size("seq") * per_device
    position = lax.axis_index("seq")
    slot_count = 2 * REACH + 1
    tube_index, owner_index = tube_tables(tube_lengths, tube_owner, blocks_all)
    ctrl_pair = lax.all_gather(jnp.stack([ctrl_key, ctrl_value]), "seq", axis=1, tiled=True)
    ctrl_keys = split_heads(ctrl_pair[0], head_width)
    ctrl_values = split_heads(ctrl_pair[1], head_width)
    ctrl_shift = ctrl_bias[:, None, None]
    key_value = jnp.stack([key_states, value_states])
    lower_side = [passed_along(key_value, "seq", distance) for distance in range(REACH, 0, -1)]
    upper_side = [passed_along(key_value, "seq", -distance) for distance in range(1, REACH + 1)]
    kv_window = lower_side + [key_value] + upper_side

    def member(slot_index, block_local, tube_id):
        block_id = (position - REACH + slot_index) * per_device + block_local
        clipped = jnp.clip(block_id, 0, blocks_all - 1)
        return (block_id >= 0) & (block_id < blocks_all) & (tube_index[clipped] == tube_id)

    def window_block(window, slot_index, block_local, member_index):
        return split_heads(
            window[slot_index][member_index, block_local * BLK : (block_local + 1) * BLK],
            head_width,
        )

    def visit_keys(update, carried, tube_id, skipped):
        for slot_index in range(slot_count):
            for key_local in range(per_device):
                if slot_index == REACH and key_local == skipped:
                    continue
                carried = lax.cond(
                    member(slot_index, key_local, tube_id),
                    partial(update, slot_index=slot_index, key_local=key_local),
                    unchanged,
                    carried,
                )
        return carried

    q_blocks, g_blocks, query_tubes, ctrl_masks = ([], [], [], [])
    query_local = 0
    q_blocks.append(split_heads(query_states, head_width))
    g_blocks.append(split_heads(d_attended, head_width))
    block_id = position * per_device + query_local
    query_tubes.append(tube_index[block_id])
    ctrl_masks.append((ctrl_owner == owner_index[block_id])[None, None, :])

    def ctrl_scores(query_local):
        return jnp.where(
            ctrl_masks[query_local],
            scores_of(q_blocks[query_local], ctrl_keys) + ctrl_shift,
            MASKED,
        )

    highs, totals, deltas, attended_blocks = ([], [], [], [])
    query_local = 0
    q_blk = q_blocks[query_local]
    own_scores = scores_of(q_blk, window_block(kv_window, REACH, query_local, 0))
    row_high = jnp.max(own_scores, axis=-1)
    statistics = (row_high, jnp.sum(jnp.exp(own_scores - row_high[..., None]), axis=-1))
    statistics = raise_stats(statistics, ctrl_scores(query_local))

    def add_stats(carried, slot_index, key_local, q_blk=q_blk):
        return raise_stats(
            carried, scores_of(q_blk, window_block(kv_window, slot_index, key_local, 0))
        )

    row_high, row_total = visit_keys(add_stats, statistics, query_tubes[query_local], query_local)
    ctrl_weights = weights_of(ctrl_scores(query_local), row_high, row_total).astype(jnp.bfloat16)
    summed = jnp.einsum(
        "hqk,khd->qhd", ctrl_weights, ctrl_values, preferred_element_type=jnp.float32
    )

    def add_values(
        carried, slot_index, key_local, q_blk=q_blk, row_high=row_high, row_total=row_total
    ):
        k_blk = window_block(kv_window, slot_index, key_local, 0)
        v_blk = window_block(kv_window, slot_index, key_local, 1)
        weights = weights_of(scores_of(q_blk, k_blk), row_high, row_total).astype(jnp.bfloat16)
        return carried + jnp.einsum(
            "hqk,khd->qhd", weights, v_blk, preferred_element_type=jnp.float32
        )

    summed = visit_keys(add_values, summed, query_tubes[query_local], -1)
    attended_blk = summed.astype(jnp.bfloat16)
    row_delta = jnp.sum(
        g_blocks[query_local].astype(jnp.float32) * attended_blk.astype(jnp.float32), axis=-1
    ).T
    highs.append(row_high)
    totals.append(row_total)
    deltas.append(row_delta)
    attended_blocks.append(attended_blk)

    def grad_terms(query_local, v_blk, scores):
        weights = weights_of(scores, highs[query_local], totals[query_local])
        d_prob = jnp.einsum(
            "qhd,khd->hqk", g_blocks[query_local], v_blk, preferred_element_type=jnp.float32
        )
        d_scores = (weights * (d_prob - deltas[query_local][..., None])).astype(jnp.bfloat16)
        return (weights.astype(jnp.bfloat16), d_scores)

    query_local = 0
    rounded, d_scores = grad_terms(query_local, ctrl_values, ctrl_scores(query_local))
    d_queries = [
        jnp.einsum("hqk,khd->qhd", d_scores, ctrl_keys, preferred_element_type=jnp.float32)
        * head_scale
    ]
    ctrl_key_grad = (
        jnp.einsum(
            "hqk,qhd->khd", d_scores, q_blocks[query_local], preferred_element_type=jnp.float32
        )
        * head_scale
    )
    ctrl_value_grad = jnp.einsum(
        "hqk,qhd->khd", rounded, g_blocks[query_local], preferred_element_type=jnp.float32
    )
    block_zeros = jnp.zeros((BLK, width_all // head_width, head_width), jnp.float32)
    key_parts = jnp.zeros((2, row_count, width_all), jnp.float32)
    for slot_index in range(slot_count):
        key_local = 0
        k_blk = window_block(kv_window, slot_index, key_local, 0)
        v_blk = window_block(kv_window, slot_index, key_local, 1)
        key_grad = block_zeros
        value_grad = block_zeros
        query_local = 0

        def add_grads(carried, query_local=query_local, k_blk=k_blk, v_blk=v_blk):
            rounded, d_scores = grad_terms(
                query_local, v_blk, scores_of(q_blocks[query_local], k_blk)
            )
            d_query_blk = (
                carried[0]
                + jnp.einsum("hqk,khd->qhd", d_scores, k_blk, preferred_element_type=jnp.float32)
                * head_scale
            )
            key_term = (
                jnp.einsum(
                    "hqk,qhd->khd",
                    d_scores,
                    q_blocks[query_local],
                    preferred_element_type=jnp.float32,
                )
                * head_scale
            )
            value_term = jnp.einsum(
                "hqk,qhd->khd", rounded, g_blocks[query_local], preferred_element_type=jnp.float32
            )
            return (d_query_blk, key_term, value_term)

        carried = lax.cond(
            member(slot_index, key_local, query_tubes[query_local]),
            add_grads,
            unchanged,
            (d_queries[query_local], key_grad, value_grad),
        )
        d_queries[query_local], key_grad, value_grad = carried
        slot_pieces = jnp.stack([key_grad, value_grad]).reshape(2, BLK, width_all)
        if slot_index == REACH:
            key_parts = key_parts + round_trip(slot_pieces)
        else:
            received = passed_along(slot_pieces.astype(jnp.bfloat16), "seq", slot_index - REACH)
            key_parts = key_parts + received.astype(jnp.float32)
    key_results = key_parts.astype(jnp.bfloat16)
    ctrl_terms = jnp.stack(
        [ctrl_key_grad.reshape(-1, width_all), ctrl_value_grad.reshape(-1, width_all)]
    )
    ctrl_results = lax.psum_scatter(ctrl_terms, "seq", scatter_dimension=1, tiled=True).astype(
        jnp.bfloat16
    )
    attended = attended_blocks[0].reshape(row_count, width_all)
    d_query = d_queries[0].reshape(row_count, width_all).astype(jnp.bfloat16)
    return (attended, d_query, key_results[0], key_results[1], ctrl_results[0], ctrl_results[1])


MESH = pl.DeviceIdType.MESH
SLOTS = (-2, -1, 1, 2)
LANES = 128
AHEAD = 2


def masked_pair(rows, low_lanes, factor):
    first = low_lanes.astype(jnp.float32) * factor
    second = factor - first
    return jnp.concatenate(
        [rows * first.astype(rows.dtype), rows * second.astype(rows.dtype)], axis=0
    )


def dot(left, right, left_dim, right_dim):
    return lax.dot_general(
        left, right, (((left_dim,), (right_dim,)), ((), ())), preferred_element_type=jnp.float32
    )


def tube_kernel(
    count, q_hbm, k_hbm, v_hbm, g_hbm, ck_hbm, cv_hbm,
    bias_hbm, length_hbm, owner_hbm, tag_hbm,
    att_ref, dq_ref, dk_ref, dv_ref, dck_ref, dcv_ref,
    q_ref, g_ref, own, window, ctrl, own_grad, grad_out, grad_mid, grad_in, ctrl_out, ctrl_mid, ctrl_in,
    bias_ref, length_ref, owner_ref, tag_ref, load_sem, query_sem,
    kv_send, kv_recv, ctrl_send, ctrl_recv, grad_send, grad_recv,
    mid_send, mid_recv, sum_send, sum_recv, part_send, part_recv,
):
    me = lax.axis_index("seq")
    column = lax.rem(me, 2)
    side = 1 - 2 * column
    peer = me + side
    near, across, far, back = 2 - column, 1 + column, 3 - 3 * column, 3 * column
    level = me // 2
    levels = count // 2
    rows = q_ref.shape[0]
    ctrl_rows = ck_hbm.shape[0]
    pairs = q_ref.shape[1] // LANES
    low_lanes = lax.broadcasted_iota(jnp.int32, (1, LANES), 1) < LANES // 2

    def inside(device):
        return (device >= 0) & (device < count)

    def columns(pair):
        return pl.ds(pl.multiple_of(pair * LANES, LANES), LANES)

    def kv_copy(pair, slot, distance):
        return pltpu.make_async_remote_copy(
            own.at[pair], window.at[pair, slot], kv_send.at[pair, slot], kv_recv.at[pair, slot],
            device_id={"seq": me - distance}, device_id_type=MESH,
        )

    def kv_arrival(pair, slot):
        return kv_copy(pair, slot, -side)

    def kv_onward(pair, by_peer):
        source, target = (far, near) if by_peer else (near, across)
        return pltpu.make_async_remote_copy(
            window.at[pair, source], window.at[pair, target],
            kv_send.at[pair, near], kv_recv.at[pair, target],
            device_id={"seq": peer if by_peer else me + 2 * side}, device_id_type=MESH,
        )

    def grad_copy(pair, slot, distance):
        return pltpu.make_async_remote_copy(
            grad_out.at[pair, slot], grad_in.at[pair, slot],
            grad_send.at[pair, slot], grad_recv.at[pair, slot],
            device_id={"seq": me + distance}, device_id_type=MESH,
        )

    def grad_arrival(pair, slot):
        return grad_copy(pair, slot, side)

    def part_copy(pair, by_peer):
        return pltpu.make_async_remote_copy(
            grad_out.at[pair, across], grad_mid.at[pair], part_send.at[pair], part_recv.at[pair],
            device_id={"seq": peer if by_peer else me - 2 * side}, device_id_type=MESH,
        )

    has_far, has_back = inside(me + 2 * side), inside(me - 2 * side)

    def by_parity(pair, act):
        even = lax.rem(pair, 3) == 0

        @pl.when(even)
        def _():
            act(True)

        @pl.when(jnp.logical_not(even))
        def _():
            act(False)

    def mate(step):
        return lax.rem(me + 2 * step, count)

    def mate_before(step):
        return lax.rem(me - 2 * step + count, count)

    def ctrl_copy(pair, step):
        return pltpu.make_async_remote_copy(
            ctrl.at[pair, me], ctrl.at[pair, me], ctrl_send.at[pair, step], ctrl_recv.at[pair, step],
            device_id={"seq": mate(step) if step else peer}, device_id_type=MESH,
        )

    def ctrl_arrival(pair, step):
        source = mate_before(step) if step else peer
        return pltpu.make_async_remote_copy(
            ctrl.at[pair, source], ctrl.at[pair, source],
            ctrl_send.at[pair, step], ctrl_recv.at[pair, step],
            device_id={"seq": source}, device_id_type=MESH,
        )

    def ctrl_onward(pair, step):
        source = mate_before(step)
        return pltpu.make_async_remote_copy(
            ctrl.at[pair, source], ctrl.at[pair, source],
            ctrl_send.at[pair, levels + step], ctrl_recv.at[pair, levels + step],
            device_id={"seq": peer}, device_id_type=MESH,
        )

    def ctrl_onward_arrival(pair, step):
        source = mate_before(step) + 1 - 2 * column
        return pltpu.make_async_remote_copy(
            ctrl.at[pair, source], ctrl.at[pair, source],
            ctrl_send.at[pair, levels + step], ctrl_recv.at[pair, levels + step],
            device_id={"seq": peer}, device_id_type=MESH,
        )

    def mid_copy(pair):
        return pltpu.make_async_remote_copy(
            ctrl_out.at[pair, 1 - column], ctrl_mid.at[pair], mid_send.at[pair], mid_recv.at[pair],
            device_id={"seq": peer}, device_id_type=MESH,
        )

    def sum_copy(pair, step):
        return pltpu.make_async_remote_copy(
            ctrl_out.at[pair, column, mate(step) // 2], ctrl_in.at[pair, level],
            sum_send.at[pair, step], sum_recv.at[pair, step],
            device_id={"seq": mate(step)}, device_id_type=MESH,
        )

    def sum_arrival(pair, step):
        source = mate_before(step)
        return pltpu.make_async_remote_copy(
            ctrl_out.at[pair, column, level], ctrl_in.at[pair, source // 2],
            sum_send.at[pair, step], sum_recv.at[pair, step],
            device_id={"seq": source}, device_id_type=MESH,
        )

    def loads(pair):
        part = columns(pair)
        return [
            pltpu.make_async_copy(source.at[:, part], target, load_sem.at[pair, i])
            for i, (source, target) in enumerate((
                (ck_hbm, ctrl.at[pair, me, 0]), (cv_hbm, ctrl.at[pair, me, 1]),
                (k_hbm, own.at[pair, 0]), (v_hbm, own.at[pair, 1]),
            ))
        ]

    def query_loads():
        return (
            pltpu.make_async_copy(q_hbm, q_ref, query_sem.at[0]),
            pltpu.make_async_copy(g_hbm, g_ref, query_sem.at[1]),
            pltpu.make_async_copy(bias_hbm, bias_ref, query_sem.at[2]),
            pltpu.make_async_copy(length_hbm, length_ref, query_sem.at[3]),
            pltpu.make_async_copy(owner_hbm, owner_ref, query_sem.at[4]),
            pltpu.make_async_copy(tag_hbm, tag_ref, query_sem.at[5]),
        )

    def start_loads(pair, _):
        for copy in loads(pair):
            copy.start()
        return 0

    lax.fori_loop(0, pairs, start_loads, 0)
    for copy in query_loads():
        copy.start()
    for slot, distance in enumerate(SLOTS):
        @pl.when(jnp.logical_not(inside(me + distance)))
        def _():
            window[:, slot] = jnp.zeros((pairs,) + window.shape[2:], window.dtype)

        @pl.when(jnp.logical_not(inside(me - distance)) | (near == slot))
        def _():
            grad_in[:, slot] = jnp.zeros((pairs,) + grad_in.shape[2:], grad_in.dtype)

    barrier = pltpu.get_barrier_semaphore()
    for partner in [peer] + [mate(step) for step in range(1, levels)]:
        pl.semaphore_signal(barrier, inc=1, device_id={"seq": partner}, device_id_type=MESH)
    pl.semaphore_wait(barrier, levels)

    def send(pair, _):
        for copy in loads(pair):
            copy.wait()
        kv_copy(pair, across, -side).start()

        @pl.when(has_far)
        def _():
            kv_copy(pair, back, -2 * side).start()

        @pl.when(has_back)
        def _():
            kv_copy(pair, far, 2 * side).start()

        for step in range(levels):
            ctrl_copy(pair, step).start()
        return 0

    lax.fori_loop(0, pairs, send, 0)

    for copy in query_loads():
        copy.wait()
    tubes = length_ref.shape[0]
    ends = []
    for tube in range(tubes):
        ends.append(length_ref[tube] + (ends[-1] if ends else 0))

    def tube_at(block):
        return sum(jnp.where(end <= block, 1, 0) for end in ends)

    mine = tube_at(me)
    owner = sum(jnp.where(mine == tube, owner_ref[tube], 0) for tube in range(tubes))
    lower2, lower, upper, upper2 = (
        inside(me + distance) & (tube_at(me + distance) == mine) for distance in SLOTS
    )
    first_bias = jnp.full((1, rows), jnp.where(lower | upper2, 0.0, MASKED), jnp.float32)
    second_bias = jnp.full((1, rows), jnp.where(upper | lower2, 0.0, MASKED), jnp.float32)
    own_bias = jnp.zeros((1, rows), jnp.float32)
    ctrl_open = tag_ref[...].reshape(1, count * ctrl_rows) == owner

    def bias_of(head):
        ctrl_bias = jnp.where(ctrl_open, bias_ref[head], MASKED)
        return jnp.concatenate([first_bias, own_bias, second_bias, ctrl_bias], axis=1)

    zero_block = jnp.zeros((rows, LANES), jnp.bfloat16)
    zero_grad = jnp.zeros((rows, LANES), jnp.float32)

    def relay(pair):
        for step in range(1, levels):
            ctrl_arrival(pair, step).wait_recv()
            ctrl_onward(pair, step).start()

        def act(by_peer):
            if not by_peer:
                kv_arrival(pair, near).wait_recv()

            @pl.when(has_far)
            def _():
                if by_peer:
                    kv_arrival(pair, far).wait_recv()
                kv_onward(pair, by_peer).start()

        by_parity(pair, act)

    def column_sums(pair):
        mid_copy(pair).wait()
        ctrl_out[pair, column] = (
            ctrl_out[pair, column].astype(jnp.float32) + ctrl_mid[pair].astype(jnp.float32)
        ).astype(jnp.bfloat16)
        for step in range(1, levels):
            sum_copy(pair, step).start()

        def act(by_peer):
            slot = far if by_peer else near

            @pl.when(has_far)
            def _():
                part_copy(pair, True).wait_recv()
                grad_out[pair, slot] = (
                    grad_out[pair, slot].astype(jnp.float32) + grad_mid[pair].astype(jnp.float32)
                ).astype(jnp.bfloat16)

            if by_peer:
                @pl.when(has_far)
                def _():
                    grad_copy(pair, far, 2 * side).start()
            else:
                grad_copy(pair, near, side).start()

        by_parity(pair, act)

    def work(pair, _):
        @pl.when(pair + AHEAD < pairs)
        def _():
            relay(pair + AHEAD)

        ctrl_arrival(pair, 0).wait_recv()
        for step in range(1, levels):
            ctrl_onward_arrival(pair, step).wait_recv()
        def await_rest(by_peer):
            if by_peer:
                kv_arrival(pair, near).wait_recv()
            else:
                @pl.when(has_far)
                def _():
                    kv_arrival(pair, far).wait_recv()

        by_parity(pair, await_rest)

        @pl.when(has_back)
        def _():
            kv_arrival(pair, back).wait_recv()
            kv_arrival(pair, across).wait_recv()

        def gathered(kind):
            first = jnp.where(
                lower, window[pair, 1, kind], jnp.where(upper2, window[pair, 3, kind], zero_block)
            )
            second = jnp.where(
                upper, window[pair, 2, kind], jnp.where(lower2, window[pair, 0, kind], zero_block)
            )
            shared = ctrl[pair, :, kind].reshape(count * ctrl_rows, LANES)
            return jnp.concatenate([first, own[pair, kind], second, shared], axis=0)

        keys = gathered(0)
        values = gathered(1)
        q_two = masked_pair(q_ref[:, columns(pair)], low_lanes, 0.125)
        g_two = masked_pair(g_ref[:, columns(pair)], low_lanes, 1.0)
        scores = dot(q_two, keys, 1, 1)
        scores = jnp.concatenate(
            [scores[:rows] + bias_of(2 * pair), scores[rows:] + bias_of(2 * pair + 1)], axis=0
        )
        raised = jnp.exp(scores - jnp.max(scores, axis=1, keepdims=True))
        weights = raised * (1.0 / jnp.sum(raised, axis=1, keepdims=True))
        rounded = weights.astype(jnp.bfloat16)
        out_two = dot(rounded, values, 1, 0)
        attended = jnp.where(low_lanes, out_two[:rows], out_two[rows:]).astype(jnp.bfloat16)
        att_ref[:, columns(pair)] = attended
        attended = attended.astype(jnp.float32)
        delta = jnp.sum(
            g_two.astype(jnp.float32) * jnp.concatenate([attended, attended], axis=0),
            axis=1, keepdims=True,
        )
        d_scores = (weights * (dot(g_two, values, 1, 1) - delta)).astype(jnp.bfloat16)
        dq_two = dot(d_scores, keys, 1, 0) * 0.125
        dq_ref[:, columns(pair)] = jnp.where(low_lanes, dq_two[:rows], dq_two[rows:]).astype(
            jnp.bfloat16
        )
        for kind, grads in enumerate((dot(d_scores, q_two, 0, 0), dot(rounded, g_two, 0, 0))):
            first, second = grads[:rows], grads[2 * rows : 3 * rows]
            own_grad[pair, kind] = grads[rows : 2 * rows].astype(jnp.bfloat16)
            for slot, (chosen, term) in enumerate(
                ((lower2, second), (lower, first), (upper, second), (upper2, first))
            ):
                grad_out[pair, slot, kind] = jnp.where(chosen, term, zero_grad).astype(jnp.bfloat16)
            shared = grads[3 * rows :].astype(jnp.bfloat16)
            for device in range(count):
                ctrl_out[pair, device % 2, device // 2, kind] = (
                    shared[device * ctrl_rows : (device + 1) * ctrl_rows]
                )
        mid_copy(pair).start()

        def hand_on(by_peer):
            @pl.when(has_back)
            def _():
                part_copy(pair, by_peer).start()
                grad_copy(pair, back, -2 * side).start()

            if by_peer:
                grad_copy(pair, near, side).start()
            else:
                @pl.when(has_far)
                def _():
                    grad_copy(pair, far, 2 * side).start()

        by_parity(pair, hand_on)

        @pl.when(pair > 0)
        def _():
            column_sums(pair - 1)

        return 0

    for pair in range(AHEAD):
        relay(pair)
    lax.fori_loop(0, pairs, work, 0)
    column_sums(pairs - 1)

    def finish(pair, _):
        ctrl_in[pair, level] = ctrl_out[pair, column, level]
        for step in range(1, levels):
            sum_arrival(pair, step).wait_recv()
        grad_arrival(pair, across).wait_recv()

        @pl.when(has_back)
        def _():
            grad_arrival(pair, far).wait_recv()

        @pl.when(has_far)
        def _():
            grad_arrival(pair, back).wait_recv()

        for kind, (key_ref, ctrl_ref) in enumerate(((dk_ref, dck_ref), (dv_ref, dcv_ref))):
            total = own_grad[pair, kind].astype(jnp.float32)
            for slot in range(len(SLOTS)):
                total += grad_in[pair, slot, kind].astype(jnp.float32)
            key_ref[:, columns(pair)] = total.astype(jnp.bfloat16)
            ctrl_total = ctrl_in[pair, 0, kind].astype(jnp.float32)
            for source in range(1, levels):
                ctrl_total += ctrl_in[pair, source, kind].astype(jnp.float32)
            ctrl_ref[:, columns(pair)] = ctrl_total.astype(jnp.bfloat16)
        return 0

    lax.fori_loop(0, pairs, finish, 0)

    def drain(pair, _):
        for step in range(levels):
            ctrl_copy(pair, step).wait_send()
        for step in range(1, levels):
            ctrl_onward(pair, step).wait_send()
            sum_copy(pair, step).wait_send()
        kv_copy(pair, across, -side).wait_send()
        grad_copy(pair, near, side).wait_send()

        @pl.when(has_far)
        def _():
            kv_copy(pair, back, -2 * side).wait_send()
            kv_onward(pair, True).wait_send()
            grad_copy(pair, far, 2 * side).wait_send()

        @pl.when(has_back)
        def _():
            kv_copy(pair, far, 2 * side).wait_send()
            part_copy(pair, True).wait_send()
            grad_copy(pair, back, -2 * side).wait_send()

        return 0

    lax.fori_loop(0, pairs, drain, 0)


def fused_shards(
    query_states, key_states, value_states, d_attended, ctrl_key, ctrl_value,
    ctrl_bias, tube_lengths, tube_owner, ctrl_owner,
):
    count = lax.axis_size("seq")
    rows, width = query_states.shape
    ctrl_rows = ctrl_key.shape[0]
    pairs = width // LANES
    vmem = pl.BlockSpec(memory_space=pltpu.VMEM)
    hbm = pl.BlockSpec(memory_space=pl.ANY)
    block = jax.ShapeDtypeStruct((rows, width), jnp.bfloat16)
    ctrl_block = jax.ShapeDtypeStruct((ctrl_rows, width), jnp.bfloat16)
    tile = (2, rows, LANES)
    ctrl_tile = (2, ctrl_rows, LANES)
    slots = len(SLOTS)
    results = pl.pallas_call(
        partial(tube_kernel, count),
        out_shape=(block, block, block, block, ctrl_block, ctrl_block),
        in_specs=[pl.BlockSpec(memory_space=pltpu.HBM)] * 10,
        out_specs=[vmem] * 6,
        scratch_shapes=[
            pltpu.VMEM((rows, width), jnp.bfloat16),
            pltpu.VMEM((rows, width), jnp.bfloat16),
            pltpu.VMEM((pairs,) + tile, jnp.bfloat16),
            pltpu.VMEM((pairs, slots) + tile, jnp.bfloat16),
            pltpu.VMEM((pairs, count) + ctrl_tile, jnp.bfloat16),
            pltpu.VMEM((pairs,) + tile, jnp.bfloat16),
            pltpu.VMEM((pairs, slots) + tile, jnp.bfloat16),
            pltpu.VMEM((pairs,) + tile, jnp.bfloat16),
            pltpu.VMEM((pairs, slots) + tile, jnp.bfloat16),
            pltpu.VMEM((pairs, 2, count // 2) + ctrl_tile, jnp.bfloat16),
            pltpu.VMEM((pairs, count // 2) + ctrl_tile, jnp.bfloat16),
            pltpu.VMEM((pairs, count // 2) + ctrl_tile, jnp.bfloat16),
            pltpu.SMEM(ctrl_bias.shape, jnp.float32),
            pltpu.SMEM(tube_lengths.shape, jnp.int32),
            pltpu.SMEM(tube_owner.shape, jnp.int32),
            pltpu.VMEM(ctrl_owner.shape, jnp.int32),
            pltpu.SemaphoreType.DMA((pairs, 4)),
            pltpu.SemaphoreType.DMA((6,)),
            pltpu.SemaphoreType.DMA((pairs, slots)),
            pltpu.SemaphoreType.DMA((pairs, slots)),
            pltpu.SemaphoreType.DMA((pairs, count)),
            pltpu.SemaphoreType.DMA((pairs, count)),
            pltpu.SemaphoreType.DMA((pairs, slots)),
            pltpu.SemaphoreType.DMA((pairs, slots)),
            pltpu.SemaphoreType.DMA((pairs,)),
            pltpu.SemaphoreType.DMA((pairs,)),
            pltpu.SemaphoreType.DMA((pairs, count // 2)),
            pltpu.SemaphoreType.DMA((pairs, count // 2)),
            pltpu.SemaphoreType.DMA((pairs,)),
            pltpu.SemaphoreType.DMA((pairs,)),
        ],
        compiler_params=pltpu.CompilerParams(
            collective_id=0, has_side_effects=True, vmem_limit_bytes=64 * 1024 * 1024 - 65536
        ),
    )(
        query_states, key_states, value_states, d_attended, ctrl_key, ctrl_value,
        ctrl_bias, tube_lengths, tube_owner, ctrl_owner,
    )
    return pl.pallas_call(
        hand_over,
        out_shape=(block, block, block, block, ctrl_block, ctrl_block),
        in_specs=[hbm] * 6,
        out_specs=[hbm] * 6,
        scratch_shapes=[pltpu.VMEM(result.shape, result.dtype) for result in results]
        + [pltpu.SemaphoreType.DMA((6,)), pltpu.SemaphoreType.DMA((6,))],
        compiler_params=pltpu.CompilerParams(vmem_limit_bytes=64 * 1024 * 1024 - 65536),
    )(*results)


def hand_over(*refs):
    loaded, load_sems, store_sems = refs[12:18], refs[18], refs[19]
    copies_in = [
        pltpu.make_async_copy(refs[i], loaded[i], load_sems.at[i]) for i in range(6)
    ]
    copies_out = [
        pltpu.make_async_copy(loaded[i], refs[6 + i], store_sems.at[i]) for i in range(6)
    ]
    for copy in copies_in:
        copy.start()
    for copy_in, copy_out in zip(copies_in, copies_out):
        copy_in.wait()
        copy_out.start()
    for copy in copies_out:
        copy.wait()


def fused_or_plain(*arrays):
    tile_rows = 16
    fits = arrays[4].shape[0] % tile_rows == 0 and arrays[0].shape[0] == BLK
    return (fused_shards if fits else shards)(*arrays)


def solution(mesh):
    return jax.shard_map(
        fused_or_plain,
        mesh=mesh,
        in_specs=(
            P(("groups", "seq"), "head"),
            P(("groups", "seq"), "head"),
            P(("groups", "seq"), "head"),
            P(("groups", "seq"), "head"),
            P(("groups", "seq"), "head"),
            P(("groups", "seq"), "head"),
            P("head"),
            P("groups"),
            P("groups"),
            P("groups"),
        ),
        out_specs=(
            P(("groups", "seq"), "head"),
            P(("groups", "seq"), "head"),
            P(("groups", "seq"), "head"),
            P(("groups", "seq"), "head"),
            P(("groups", "seq"), "head"),
            P(("groups", "seq"), "head"),
        ),
        check_vma=False,
    )
```
